512 devices in a mesh: dp: 32 (over z_lo, y), tensor: 16 (over x, z_hi, core).
Axes of the slice: x: 4, y: 4, z: 16 (z_hi: 2, z_lo: 8; z = z_hi * 8 + z_lo), core: 2. Of those that a mesh axis runs over, the one named last changes fastest.
Arguments:
- tokens: bfloat16 [15360, 4096], P('dp'), may hold values from -6 to 6
- gate_weight: bfloat16 [4096, 14336], P('dp', 'tensor'), may hold values from -0.09375 to 0.09375
- up_weight: bfloat16 [4096, 14336], P('dp', 'tensor'), may hold values from -0.09375 to 0.09375
- out_grad: bfloat16 [15360, 4096], P('dp', 'tensor'), may hold values from -6 to 6
- in_factor: bfloat16 [14336, 64], P('tensor'), may hold values from -0.046875 to 0.046875
- out_factor: bfloat16 [4096, 64], P('tensor'), may hold values from -0.09375 to 0.09375
- queries: bfloat16 [1024, 4096], P('dp', 'tensor'), may hold values from -6 to 6
Outputs:
- scores: float32 [1024, 96], P('dp')
The draws below stay inside these ranges and needn't reach their ends.
All inputs are finite; a program needn't handle non-finite values.
Results may differ from the reference program's by a relative error of at most 0.003.
Values may be sent and summed in bfloat16 or wider, within the bound.
No kernel may reach another device: no remote copies, remote signals or barrier semaphores. Data moves between devices by JAX's collectives and lax.ppermute only.
A program may use at most 64 MiB of HBM per device.

```python
import jax
import jax.numpy as jnp
from jax import lax

D = 4096
FF = 14336
RANK = 64
LEN = 160
QUERIES = 1024
FEAT = 4096
TOKENS = 15360


def block_scale(rng, dims, shards, smallest, top_value):
    loudness = 1.0
    for axis_at, shards_of in shards:
        heights = jax.random.uniform(jax.random.fold_in(jax.random.fold_in(rng, 6), axis_at), (shards_of,), jnp.float32, smallest / len(shards), top_value / len(shards))
        loudness = loudness * jnp.repeat(jnp.exp(heights), dims[axis_at] // shards_of).reshape((-1,) + (1,) * (len(dims) - 1 - axis_at))
    return loudness


def gaussian(rng, dims, scale, reach, split=(), kind=jnp.bfloat16):
    values = scale * jax.random.normal(rng, dims, jnp.float32)
    if split:
        values = values * block_scale(rng, dims, split, -0.22, 0.18)
    return jnp.clip(values, -reach, reach).astype(kind)


def setup_inputs(seed: int = 0) -> dict:
    seeds = jax.random.split(jax.random.key(seed), 8)
    return {
        "tokens": gaussian(seeds[0], (TOKENS, D), 1.0, 6.0, ((0, 32),)),
        "gate_weight": gaussian(seeds[1], (D, FF), D ** -0.5, 0.09375, ((0, 32), (1, 16))),
        "up_weight": gaussian(seeds[2], (D, FF), D ** -0.5, 0.09375, ((0, 32), (1, 16))),
        "out_grad": gaussian(seeds[3], (TOKENS, D), 1.0, 6.0, ((0, 32), (1, 16))),
        "in_factor": gaussian(seeds[4], (FF, RANK), FF ** -0.5, 0.046875, ((0, 16),)),
        "out_factor": gaussian(seeds[5], (D, RANK), D ** -0.5, 0.09375, ((0, 16),)),
        "queries": gaussian(seeds[6], (QUERIES, FEAT), 1.0, 6.0, ((0, 32), (1, 16))),
    }


damping = 0.1

def solve_kernel(kernel, cross):
    factor = jnp.linalg.cholesky(kernel)
    lower_solved = lax.linalg.triangular_solve(factor, cross.T, left_side=True, lower=True)
    result = lax.linalg.triangular_solve(factor, lower_solved, left_side=True, lower=True, transpose_a=True)
    return result.T

def reference(tokens, gate_weight, up_weight, out_grad, in_factor, out_factor, queries):
    count = tokens.shape[0] // LEN
    token_seqs = tokens.reshape(count, LEN, tokens.shape[1])
    grad_seqs = out_grad.reshape(count, LEN, out_grad.shape[1])

    def one_sequence(pair):
        inputs, grads = pair
        gate = jnp.dot(inputs.astype(jnp.float32), gate_weight.astype(jnp.float32), preferred_element_type=jnp.float32)
        up = jnp.dot(inputs.astype(jnp.float32), up_weight.astype(jnp.float32), preferred_element_type=jnp.float32)
        hidden = (jax.nn.silu(gate) * up).astype(jnp.bfloat16)
        in_proj = jnp.dot(hidden.astype(jnp.float32), in_factor.astype(jnp.float32), preferred_element_type=jnp.float32)
        out_proj = jnp.dot(grads.astype(jnp.float32), out_factor.astype(jnp.float32), preferred_element_type=jnp.float32)
        outer = jnp.dot(in_proj.T.astype(jnp.float32), out_proj.astype(jnp.float32), precision=lax.Precision.HIGHEST, preferred_element_type=jnp.float32)
        return outer.reshape(-1) / jnp.sqrt(jnp.float32(LEN))
    features = lax.map(one_sequence, (token_seqs, grad_seqs))
    width = features.shape[1]
    kernel = jnp.dot(features, features.T, precision=lax.Precision.HIGHEST) / width
    kernel = kernel + damping * jnp.eye(count, dtype=jnp.float32)
    cross = jnp.dot(queries.astype(jnp.float32), features.T, precision=lax.Precision.HIGHEST) / jnp.sqrt(jnp.float32(width))
    return solve_kernel(kernel, cross)
```

```python
import functools

import jax
import jax.numpy as jnp
from jax import lax
from jax.experimental import pallas as pl
from jax.experimental.pallas import tpu as pltpu
from jax.sharding import Mesh, PartitionSpec as P

LEN = 160
DAMPING = 0.1
ZL, Y, X, ZH, C = 8, 4, 4, 2, 2
PLANE = ("y", "x", "c")
HIGHEST = lax.Precision.HIGHEST


def solve_body(features_ref, queries_ref, out_ref):
    blocks, count, width = features_ref.shape
    total = blocks * width
    features = jnp.concatenate([features_ref[d] for d in range(blocks)], axis=1)
    both = jnp.concatenate([features, queries_ref[...]], axis=0)
    system = lax.dot_general(
        features, both, (((1,), (1,)), ((), ())), preferred_element_type=jnp.float32
    )
    row = lax.broadcasted_iota(jnp.int32, system.shape, 0)
    lane = lax.broadcasted_iota(jnp.int32, system.shape, 1)
    system = jnp.where(
        lane < count,
        system / total + jnp.where(row == lane, DAMPING, 0.0),
        system / (total**0.5),
    )
    groups = [system[8 * g : 8 * g + 8] for g in range(count // 8)]
    inner = lax.broadcasted_iota(jnp.int32, groups[0].shape, 0)
    for k in range(count):
        g, r = k // 8, k % 8
        pivot_row = groups[g][r : r + 1]
        scaled = pivot_row / pivot_row[:, k : k + 1]
        updated = [block - block[:, k : k + 1] * scaled for block in groups]
        updated[g] = jnp.where(inner == r, scaled, updated[g])
        groups = updated
    width = system.shape[1]
    groups += [jnp.zeros_like(groups[0])] * (width // 8 - len(groups))
    solved = jnp.concatenate(groups, axis=0).T
    out_ref[...] = solved[count:, :count]


def solve(features, queries):
    count = features.shape[1]
    return pl.pallas_call(
        solve_body,
        out_shape=jax.ShapeDtypeStruct((queries.shape[0], count), jnp.float32),
        compiler_params=pltpu.CompilerParams(vmem_limit_bytes=32 * 2**20),
        name="solve",
    )(features, queries)


def share(x, axes, count):
    return lax.all_to_all(
        jnp.broadcast_to(x[None], (count,) + x.shape), axes, 0, 0, tiled=True
    )


def layer_kernel(place_ref, factor_ref, *refs):
    chains = 2 * ZL - 1
    blocks = refs[:chains]
    all_tokens, out_ref, weights, tokens, token_sems = refs[chains:]
    z = place_ref[0]
    hidden = blocks[0].shape[1] // 2
    half = all_tokens.shape[1]

    def token_copies(p):
        for c in range(2):
            yield pltpu.make_async_copy(
                all_tokens.at[2 * p + c], tokens.at[p, pl.ds(c * half, half)], token_sems.at[p, c]
            )

    for p in range(Y):
        for copy in token_copies(p):
            copy.start()

    gap = jnp.zeros((256 - hidden, 128), jnp.bfloat16)

    def place_block(at, owner):
        for k in range(Y):
            block = blocks[at][k]
            wide = jnp.concatenate([block[:hidden], gap, block[hidden:], gap], axis=0)
            weights[pl.ds(pl.multiple_of((owner * Y + k) * 128, 128), 128), :] = wide.T

    place_block(0, z)
    for s in range(1, ZL):
        @pl.when(z >= s)
        def _():
            place_block(s, z - s)

        @pl.when(z + s < ZL)
        def _():
            place_block(s + ZL - 1, z + s)

    def part(p, carry):
        for copy in token_copies(p):
            copy.wait()
        both = jnp.dot(tokens[p], weights[...], preferred_element_type=jnp.float32)
        gate, up = both[:, :256], both[:, 256:]
        value = (gate / (1.0 + jnp.exp(-gate)) * up).astype(jnp.bfloat16)
        proj = lax.dot_general(
            factor_ref[...], value, (((1,), (1,)), ((), ())),
            preferred_element_type=jnp.float32,
        )
        space = jnp.zeros((proj.shape[0], 256 - half), jnp.float32)
        proj = jnp.concatenate([proj[:, :half], space, proj[:, half:], space], axis=1)
        lanes = pl.ds(pl.multiple_of(p * 512, 512), 512)
        for d in range(out_ref.shape[0]):
            out_ref[d, :, lanes] = proj[2 * d : 2 * d + 2]
        return carry

    lax.fori_loop(0, Y, part, 0)


def layer(place, factor, blocks, tokens):
    _, half, depth = tokens.shape
    cols = blocks[0].shape[1]
    rank = factor.shape[0]
    vmem = pl.BlockSpec(memory_space=pltpu.VMEM)
    return pl.pallas_call(
        layer_kernel,
        out_shape=jax.ShapeDtypeStruct((rank // 2, 2, Y * 512), jnp.float32),
        in_specs=[pl.BlockSpec(memory_space=pltpu.SMEM)]
        + [vmem] * (1 + len(blocks))
        + [pl.BlockSpec(memory_space=pl.ANY)],
        out_specs=vmem,
        scratch_shapes=[
            pltpu.VMEM((depth, 512), jnp.bfloat16),
            pltpu.VMEM((Y, 2 * half, depth), jnp.bfloat16),
            pltpu.SemaphoreType.DMA((Y, 2)),
        ],
        compiler_params=pltpu.CompilerParams(vmem_limit_bytes=44 * 2**20),
        cost_estimate=pl.CostEstimate(
            flops=4 * Y * half * cols * depth,
            bytes_accessed=2 * depth * (cols + 2 * Y * half),
            transcendentals=0,
        ),
        name="layer",
    )(place, factor, *blocks, tokens)


def tie(value, *after):
    return lax.optimization_barrier((value,) + after)[0]


class Chain:
    def __init__(self, block):
        self.ups, self.downs = [block], [block]

    def step(self):
        s = len(self.ups)
        up, down = self.ups[-1], self.downs[-1]
        if s > 2:
            up, down = tie(up, self.downs[-2]), tie(down, self.ups[-2])
        self.ups.append(lax.ppermute(up, "zl", [(z, z + 1) for z in range(s - 1, ZL - 1)]))
        self.downs.append(lax.ppermute(down, "zl", [(z, z - 1) for z in range(1, ZL + 1 - s)]))

    def hold(self, value):
        self.ups[-1], value = lax.optimization_barrier((self.ups[-1], value))
        return value

    def blocks(self):
        return self.ups + self.downs[1:]


def weight_quarters(gate_weight, up_weight):
    depth, cols = gate_weight.shape
    return jnp.concatenate(
        [w.T.reshape(Y, cols // Y, depth) for w in (gate_weight, up_weight)], axis=1
    )


def out_partial(out_grad, out_factor):
    half = out_grad.shape[0] // 2
    grads = jnp.pad(out_grad.reshape(2, half, -1), ((0, 0), (0, 256 - half), (0, 0)))
    return lax.dot_general(
        out_factor, grads.reshape(512, -1), (((0,), (1,)), ((), ())),
        preferred_element_type=jnp.float32,
    )


def scatter_out_share_queries(out, queries):
    count = X * C
    rank, lanes = out.shape
    ours = queries.astype(jnp.float32).reshape(-1, lanes)
    sent = jnp.concatenate(
        [out.reshape(count, rank // count, lanes), jnp.broadcast_to(ours, (count,) + ours.shape)],
        axis=1,
    )
    got = lax.all_to_all(sent, ("x", "c"), 0, 0, tiled=True)
    full = got[:, rank // count :].reshape((count,) + queries.shape).astype(queries.dtype)
    return got[:, : rank // count].sum(0), full


def shards(tokens, gate_weight, up_weight, out_grad, in_factor, out_factor, queries):
    rows = tokens.shape[0]
    rank = in_factor.shape[1]
    half = rows // 2
    z, y, c = (lax.axis_index(name) for name in ("zl", "y", "c"))
    mine = lax.dynamic_slice_in_dim(tokens, c * half, half, 0)
    plane_tokens = lax.all_gather(mine, ("y", "c"))
    quarter = in_factor.shape[0] // Y
    factor = lax.dynamic_slice_in_dim(in_factor, y * quarter, quarter, 0).T
    factor = jnp.pad(factor, ((0, 0), (0, 256 - quarter)))

    quarters = weight_quarters(gate_weight, up_weight)
    chain = Chain(lax.all_to_all(quarters, "y", 0, 0, tiled=True))
    out = out_partial(out_grad, out_factor)
    for s in range(1, ZL):
        chain.step()
        if s == 1:
            out = tie(out, chain.ups[-1])
            out, plane_queries = scatter_out_share_queries(out, queries)
        if s == 3:
            out, plane_queries = chain.hold((out, plane_queries))
        if s == 6:
            plane_tokens = chain.hold(plane_tokens)
    out = lax.all_gather(tie(out, plane_tokens), "zh").sum(0)
    query_rows = lax.all_gather(tie(plane_queries, out), "zh")
    out = share(out, PLANE, Y * X * C)
    out = out.reshape(Y, rank, -1).transpose(1, 0, 2).reshape(rank, -1)

    place = jnp.stack([z]).astype(jnp.int32)
    in_part = layer(place, factor, chain.blocks(), plane_tokens)
    query_rows = tie(query_rows, in_part)
    query_rows = query_rows.reshape((ZH, X, C) + queries.shape).transpose(3, 1, 0, 2, 4)
    query_rows = query_rows.reshape(queries.shape[0], -1)
    in_proj = lax.all_to_all(in_part, PLANE, 0, 0, tiled=True).sum(0)

    seqs = Y * rows // LEN
    lane = jnp.arange(in_proj.shape[1])
    token = lane // 256 * half + lane % 256
    mask = (token // LEN)[None, :] == jnp.arange(seqs)[:, None]
    spread = jnp.where(mask[:, None, :], in_proj[None], 0.0).reshape(2 * seqs, -1)
    fragment = jnp.dot(spread, out.T, precision=HIGHEST) / jnp.sqrt(jnp.float32(LEN))
    fragment = fragment.reshape(seqs, 2 * rank)
    columns = share(fragment, ("zh", "zl"), ZH * ZL)
    columns = columns.reshape(ZH, ZL * seqs, 2 * rank).sum(0).astype(jnp.bfloat16)
    features = share(columns, PLANE, Y * X * C)
    return solve(features, query_rows)


def solution(mesh):
    fine = Mesh(mesh.devices.reshape(ZL, Y, X, ZH, C), ("zl", "y", "x", "zh", "c"))
    dp, tensor = ("zl", "y"), ("x", "zh", "c")
    in_specs = (
        P(dp, None),
        P(dp, tensor),
        P(dp, tensor),
        P(dp, tensor),
        P(tensor, None),
        P(tensor, None),
        P(dp, tensor),
    )
    return jax.shard_map(
        shards, mesh=fine, in_specs=in_specs, out_specs=P(dp, None), check_vma=False
    )
```

```python
import functools

import jax
import jax.numpy as jnp
from jax import lax
from jax.experimental import pallas as pl
from jax.experimental.pallas import tpu as pltpu
from jax.sharding import Mesh, PartitionSpec as P

LEN = 160
DAMPING = 0.1
ZL, Y, X, ZH, C = 8, 4, 4, 2, 2
PLANE = ("y", "x", "c")
HIGHEST = lax.Precision.HIGHEST


def solve_body(features_ref, queries_ref, out_ref):
    blocks, count, width = features_ref.shape
    total = blocks * width
    features = jnp.concatenate([features_ref[d] for d in range(blocks)], axis=1)
    both = jnp.concatenate([features, queries_ref[...]], axis=0)
    system = lax.dot_general(
        features, both, (((1,), (1,)), ((), ())), preferred_element_type=jnp.float32
    )
    row = lax.broadcasted_iota(jnp.int32, system.shape, 0)
    lane = lax.broadcasted_iota(jnp.int32, system.shape, 1)
    system = jnp.where(
        lane < count,
        system / total + jnp.where(row == lane, DAMPING, 0.0),
        system / (total**0.5),
    )
    on_diagonal = jnp.where(row == lane, system, 0.0)
    row_scale = lax.rsqrt(jnp.sum(on_diagonal, axis=1, keepdims=True))
    lane_scale = jnp.sum(jnp.where(row == lane, row_scale, 0.0), axis=0, keepdims=True)
    system = system * row_scale * jnp.where(lane < count, lane_scale, 1.0)
    groups = [system[8 * g : 8 * g + 8] for g in range(count // 8)]
    inner = lax.broadcasted_iota(jnp.int32, groups[0].shape, 0)
    for k in range(0, count, 2):
        g, r = k // 8, k % 8
        p, q = groups[g][r : r + 1], groups[g][r + 1 : r + 2]
        a, b, c, d = p[:, k : k + 1], p[:, k + 1 : k + 2], q[:, k : k + 1], q[:, k + 1 : k + 2]
        inverse = 1.0 / (a * d - b * c)
        first = (d * inverse) * p - (b * inverse) * q
        second = (a * inverse) * q - (c * inverse) * p
        updated = [
            block - block[:, k : k + 1] * first - block[:, k + 1 : k + 2] * second
            for block in groups
        ]
        updated[g] = jnp.where(
            inner == r, first, jnp.where(inner == r + 1, second, updated[g])
        )
        groups = updated
    groups = [block * row_scale[8 * g : 8 * g + 8] for g, block in enumerate(groups)]
    width = system.shape[1]
    groups += [jnp.zeros_like(groups[0])] * (width // 8 - len(groups))
    solved = jnp.concatenate(groups, axis=0).T
    out_ref[...] = solved[count:, :count]


def solve(features, queries):
    count = features.shape[1]
    return pl.pallas_call(
        solve_body,
        out_shape=jax.ShapeDtypeStruct((queries.shape[0], count), jnp.float32),
        compiler_params=pltpu.CompilerParams(vmem_limit_bytes=32 * 2**20),
        name="solve",
    )(features, queries)


def share(x, axes, count):
    return lax.all_to_all(
        jnp.broadcast_to(x[None], (count,) + x.shape), axes, 0, 0, tiled=True
    )


def layer_kernel(place_ref, factor_ref, *refs):
    chains = 2 * ZL - 1
    blocks = refs[:chains]
    all_tokens, out_ref, weights, tokens, token_sems = refs[chains:]
    z = place_ref[0]
    hidden = blocks[0].shape[1] // 2
    half = all_tokens.shape[1]

    def token_copies(p):
        for c in range(2):
            yield pltpu.make_async_copy(
                all_tokens.at[2 * p + c], tokens.at[p, pl.ds(c * half, half)], token_sems.at[p, c]
            )

    for p in range(Y):
        for copy in token_copies(p):
            copy.start()

    gap = jnp.zeros((256 - hidden, 128), jnp.bfloat16)

    def place_block(at, owner):
        for k in range(Y):
            block = blocks[at][k]
            wide = jnp.concatenate([block[:hidden], gap, block[hidden:], gap], axis=0)
            weights[pl.ds(pl.multiple_of((owner * Y + k) * 128, 128), 128), :] = wide.T

    place_block(0, z)
    for s in range(1, ZL):
        @pl.when(z >= s)
        def _():
            place_block(s, z - s)

        @pl.when(z + s < ZL)
        def _():
            place_block(s + ZL - 1, z + s)

    def part(p, carry):
        for copy in token_copies(p):
            copy.wait()
        both = jnp.dot(tokens[p], weights[...], preferred_element_type=jnp.float32)
        gate, up = both[:, :256], both[:, 256:]
        value = (gate / (1.0 + jnp.exp(-gate)) * up).astype(jnp.bfloat16)
        proj = lax.dot_general(
            factor_ref[...], value, (((1,), (1,)), ((), ())),
            preferred_element_type=jnp.float32,
        )
        space = jnp.zeros((proj.shape[0], 256 - half), jnp.float32)
        proj = jnp.concatenate([proj[:, :half], space, proj[:, half:], space], axis=1)
        lanes = pl.ds(pl.multiple_of(p * 512, 512), 512)
        for d in range(out_ref.shape[0]):
            out_ref[d, :, lanes] = proj[2 * d : 2 * d + 2]
        return carry

    lax.fori_loop(0, Y, part, 0)


def layer(place, factor, blocks, tokens):
    _, half, depth = tokens.shape
    cols = blocks[0].shape[1]
    rank = factor.shape[0]
    vmem = pl.BlockSpec(memory_space=pltpu.VMEM)
    return pl.pallas_call(
        layer_kernel,
        out_shape=jax.ShapeDtypeStruct((rank // 2, 2, Y * 512), jnp.float32),
        in_specs=[pl.BlockSpec(memory_space=pltpu.SMEM)]
        + [vmem] * (1 + len(blocks))
        + [pl.BlockSpec(memory_space=pl.ANY)],
        out_specs=vmem,
        scratch_shapes=[
            pltpu.VMEM((depth, 512), jnp.bfloat16),
            pltpu.VMEM((Y, 2 * half, depth), jnp.bfloat16),
            pltpu.SemaphoreType.DMA((Y, 2)),
        ],
        compiler_params=pltpu.CompilerParams(vmem_limit_bytes=38 * 2**20),
        cost_estimate=pl.CostEstimate(
            flops=4 * Y * half * cols * depth,
            bytes_accessed=2 * depth * (cols + 2 * Y * half),
            transcendentals=0,
        ),
        name="layer",
    )(place, factor, *blocks, tokens)


def tie(value, *after):
    return lax.optimization_barrier((value,) + after)[0]


class Chain:
    def __init__(self, block):
        self.ups, self.downs = [block], [block]

    def step(self):
        s = len(self.ups)
        up, down = self.ups[-1], self.downs[-1]
        if s > 2:
            up, down = tie(up, self.downs[-2]), tie(down, self.ups[-2])
        self.ups.append(lax.ppermute(up, "zl", [(z, z + 1) for z in range(s - 1, ZL - 1)]))
        self.downs.append(lax.ppermute(down, "zl", [(z, z - 1) for z in range(1, ZL + 1 - s)]))

    def after(self, *values):
        self.ups[-1] = tie(self.ups[-1], *values)
        self.downs[-1] = tie(self.downs[-1], *values)

    def blocks(self):
        return self.ups + self.downs[1:]


def weight_quarters(gate_weight, up_weight):
    depth, cols = gate_weight.shape
    return jnp.concatenate(
        [w.T.reshape(Y, cols // Y, depth) for w in (gate_weight, up_weight)], axis=1
    )


def out_partial(out_grad, out_factor):
    half = out_grad.shape[0] // 2
    grads = jnp.pad(out_grad.reshape(2, half, -1), ((0, 0), (0, 256 - half), (0, 0)))
    return lax.dot_general(
        out_factor, grads.reshape(512, -1), (((0,), (1,)), ((), ())),
        preferred_element_type=jnp.float32,
    )


def exchange_z(out, queries):
    rows, cols = queries.shape
    high = lax.reduce_precision(out, 8, 7)
    sent = jnp.concatenate(
        [v.astype(jnp.bfloat16) for v in (high, out - high)] + [queries.reshape(-1, out.shape[1])]
    )
    got = lax.all_gather(sent, "zh")
    count = out.shape[0]
    parts = got[:, : 2 * count].astype(jnp.float32)
    out = (parts[:, :count] + parts[:, count:]).sum(0)
    return out, got[:, 2 * count :].reshape(ZH, rows, cols)


def share_plane(out, queries):
    high = lax.reduce_precision(out, 8, 7)
    sent = jnp.concatenate(
        [v.astype(jnp.bfloat16) for v in (high, out - high)]
        + [queries.reshape(-1, out.shape[1])]
    )
    return share(sent, PLANE, Y * X * C)


def unpack_plane(got, count, rows, cols):
    lanes = got.shape[2]
    parts = got[:, : 2 * count].astype(jnp.float32)
    out = (parts[:, :count] + parts[:, count:]).reshape(Y, X * C * count, lanes)
    here = got.reshape((Y, X * C) + got.shape[1:])
    here = lax.dynamic_index_in_dim(here, lax.axis_index("y"), 0, keepdims=False)
    queries = here[:, 2 * count :].reshape(X, C, ZH, rows, cols)
    queries = queries.transpose(3, 0, 2, 1, 4).reshape(rows, -1)
    return out.transpose(1, 0, 2).reshape(X * C * count, Y * lanes), queries


def shards(tokens, gate_weight, up_weight, out_grad, in_factor, out_factor, queries):
    rows = tokens.shape[0]
    rank = in_factor.shape[1]
    half = rows // 2
    z, y, c = (lax.axis_index(name) for name in ("zl", "y", "c"))
    mine = lax.dynamic_slice_in_dim(tokens, c * half, half, 0)
    plane_tokens = lax.all_gather(mine, ("y", "c"))
    quarter = in_factor.shape[0] // Y
    factor = lax.dynamic_slice_in_dim(in_factor, y * quarter, quarter, 0).T
    factor = jnp.pad(factor, ((0, 0), (0, 256 - quarter)))

    quarters = weight_quarters(gate_weight, up_weight)
    chain = Chain(lax.all_to_all(quarters, "y", 0, 0, tiled=True))
    out = out_partial(out_grad, out_factor)
    for s in range(1, ZL):
        chain.step()
        if s == 2:
            out = tie(out, chain.ups[-1]).reshape(X * C, rank // (X * C), -1)
            out = lax.all_to_all(out, ("x", "c"), 0, 0, tiled=True).sum(0)
        if s == 4:
            chain.after(out)
            out = tie(out, chain.ups[-1])
            out, query_rows = exchange_z(out, queries)
        if s == 6:
            chain.after(out, query_rows)
            out = tie(out, chain.ups[-1])
            shared = share_plane(out, query_rows)

    place = jnp.stack([z]).astype(jnp.int32)
    in_part = layer(place, factor, chain.blocks(), plane_tokens)
    shared, in_part = lax.optimization_barrier((shared, in_part))
    out, query_rows = unpack_plane(shared, rank // (X * C), *queries.shape)
    in_proj = lax.all_to_all(in_part, PLANE, 0, 0, tiled=True)
    in_proj = in_proj.sum(0)

    seqs = Y * rows // LEN
    lane = jnp.arange(in_proj.shape[1])
    token = lane // 256 * half + lane % 256
    mask = (token // LEN)[None, :] == jnp.arange(seqs)[:, None]
    spread = jnp.where(mask[:, None, :], in_proj[None], 0.0).reshape(2 * seqs, -1)
    fragment = jnp.dot(spread, out.T, precision=HIGHEST) / jnp.sqrt(jnp.float32(LEN))
    fragment = fragment.reshape(seqs, 2 * rank)
    columns = share(fragment, ("zh", "zl"), ZH * ZL)
    columns = columns.reshape(ZH, ZL * seqs, 2 * rank).sum(0).astype(jnp.bfloat16)
    features = share(columns, PLANE, Y * X * C)
    return solve(features, query_rows)


def solution(mesh):
    fine = Mesh(mesh.devices.reshape(ZL, Y, X, ZH, C), ("zl", "y", "x", "zh", "c"))
    dp, tensor = ("zl", "y"), ("x", "zh", "c")
    in_specs = (
        P(dp, None),
        P(dp, tensor),
        P(dp, tensor),
        P(dp, tensor),
        P(tensor, None),
        P(tensor, None),
        P(dp, tensor),
    )
    return jax.shard_map(
        shards, mesh=fine, in_specs=in_specs, out_specs=P(dp, None), check_vma=False
    )
```

```python
import functools

import jax
import jax.numpy as jnp
from jax import lax
from jax.experimental import pallas as pl
from jax.experimental.pallas import tpu as pltpu
from jax.sharding import Mesh, PartitionSpec as P

LEN = 160
DAMPING = 0.1
ZL, Y, X, ZH, C = 8, 4, 4, 2, 2
PLANE = ("y", "x", "c")
HIGHEST = lax.Precision.HIGHEST


def solve_body(features_ref, queries_ref, out_ref):
    blocks, count, width = features_ref.shape
    total = blocks * width
    features = jnp.concatenate([features_ref[d] for d in range(blocks)], axis=1)
    both = jnp.concatenate([features, queries_ref[...]], axis=0)
    system = lax.dot_general(
        features, both, (((1,), (1,)), ((), ())), preferred_element_type=jnp.float32
    )
    row = lax.broadcasted_iota(jnp.int32, system.shape, 0)
    lane = lax.broadcasted_iota(jnp.int32, system.shape, 1)
    system = jnp.where(
        lane < count,
        system / total + jnp.where(row == lane, DAMPING, 0.0),
        system / (total**0.5),
    )
    on_diagonal = jnp.where(row == lane, system, 0.0)
    row_scale = lax.rsqrt(jnp.sum(on_diagonal, axis=1, keepdims=True))
    lane_scale = jnp.sum(jnp.where(row == lane, row_scale, 0.0), axis=0, keepdims=True)
    system = system * row_scale * jnp.where(lane < count, lane_scale, 1.0)
    groups = [system[8 * g : 8 * g + 8] for g in range(count // 8)]
    inner = lax.broadcasted_iota(jnp.int32, groups[0].shape, 0)
    whole = groups[0].shape
    side = 4
    for low in range(0, len(groups), side):
        inside = groups[low : low + side]
        for k in range(8 * low, 8 * (low + side), 2):
            g, r = k // 8 - low, k % 8
            p = jnp.broadcast_to(inside[g][r : r + 1], whole)
            q = jnp.broadcast_to(inside[g][r + 1 : r + 2], whole)
            a, b, c, d = (
                jnp.broadcast_to(v[:, n : n + 1], whole) for v in (p, q) for n in (k, k + 1)
            )
            inverse = 1.0 / (a * d - b * c)
            first = (d * inverse) * p - (b * inverse) * q
            second = (a * inverse) * q - (c * inverse) * p
            updated = [
                block
                - jnp.broadcast_to(block[:, k : k + 1], whole) * first
                - jnp.broadcast_to(block[:, k + 1 : k + 2], whole) * second
                for block in inside
            ]
            updated[g] = jnp.where(
                inner == r, first, jnp.where(inner == r + 1, second, updated[g])
            )
            inside = updated
        rest = jnp.concatenate(groups[:low] + groups[low + side :], axis=0)
        rest = rest - lax.dot_general(
            rest[:, 8 * low : 8 * (low + side)], jnp.concatenate(inside, axis=0),
            (((1,), (0,)), ((), ())),
            precision=HIGHEST, preferred_element_type=jnp.float32,
        )
        rest = [rest[8 * n : 8 * n + 8] for n in range(len(groups) - side)]
        groups = rest[:low] + inside + rest[low:]
    groups = [block * row_scale[8 * g : 8 * g + 8] for g, block in enumerate(groups)]
    width = system.shape[1]
    groups += [jnp.zeros_like(groups[0])] * (width // 8 - len(groups))
    solved = jnp.concatenate(groups, axis=0).T
    out_ref[...] = solved[count:, :count]


def solve(features, queries):
    count = features.shape[1]
    return pl.pallas_call(
        solve_body,
        out_shape=jax.ShapeDtypeStruct((queries.shape[0], count), jnp.float32),
        compiler_params=pltpu.CompilerParams(vmem_limit_bytes=32 * 2**20),
        name="solve",
    )(features, queries)


def share(x, axes, count):
    return lax.all_to_all(
        jnp.broadcast_to(x[None], (count,) + x.shape), axes, 0, 0, tiled=True
    )


def layer_kernel(place_ref, factor_ref, *refs):
    chains = 2 * ZL - 1
    blocks = refs[:chains]
    all_tokens, out_ref, weights, tokens, token_sems = refs[chains:]
    z = place_ref[0]
    hidden = blocks[0].shape[1] // 2
    half = all_tokens.shape[1]

    def token_copies(p):
        for c in range(2):
            yield pltpu.make_async_copy(
                all_tokens.at[2 * p + c], tokens.at[p, pl.ds(c * half, half)], token_sems.at[p, c]
            )

    for p in range(Y):
        for copy in token_copies(p):
            copy.start()

    gap = jnp.zeros((256 - hidden, 128), jnp.bfloat16)

    def place_block(at, owner):
        for k in range(Y):
            block = blocks[at][k]
            wide = jnp.concatenate([block[:hidden], gap, block[hidden:], gap], axis=0)
            weights[pl.ds(pl.multiple_of((owner * Y + k) * 128, 128), 128), :] = wide.T

    place_block(0, z)
    for s in range(1, ZL):
        @pl.when(z >= s)
        def _():
            place_block(s, z - s)

        @pl.when(z + s < ZL)
        def _():
            place_block(s + ZL - 1, z + s)

    def part(p, carry):
        for copy in token_copies(p):
            copy.wait()
        both = jnp.dot(tokens[p], weights[...], preferred_element_type=jnp.float32)
        gate, up = both[:, :256], both[:, 256:]
        value = (gate / (1.0 + jnp.exp(-gate)) * up).astype(jnp.bfloat16)
        proj = lax.dot_general(
            factor_ref[...], value, (((1,), (1,)), ((), ())),
            preferred_element_type=jnp.float32,
        )
        space = jnp.zeros((proj.shape[0], 256 - half), jnp.float32)
        proj = jnp.concatenate([proj[:, :half], space, proj[:, half:], space], axis=1)
        lanes = pl.ds(pl.multiple_of(p * 512, 512), 512)
        for d in range(out_ref.shape[0]):
            out_ref[d, :, lanes] = proj[2 * d : 2 * d + 2]
        return carry

    lax.fori_loop(0, Y, part, 0)


def layer(place, factor, blocks, tokens):
    _, half, depth = tokens.shape
    cols = blocks[0].shape[1]
    rank = factor.shape[0]
    vmem = pl.BlockSpec(memory_space=pltpu.VMEM)
    return pl.pallas_call(
        layer_kernel,
        out_shape=jax.ShapeDtypeStruct((rank // 2, 2, Y * 512), jnp.float32),
        in_specs=[pl.BlockSpec(memory_space=pltpu.SMEM)]
        + [vmem] * (1 + len(blocks))
        + [pl.BlockSpec(memory_space=pl.ANY)],
        out_specs=vmem,
        scratch_shapes=[
            pltpu.VMEM((depth, 512), jnp.bfloat16),
            pltpu.VMEM((Y, 2 * half, depth), jnp.bfloat16),
            pltpu.SemaphoreType.DMA((Y, 2)),
        ],
        compiler_params=pltpu.CompilerParams(vmem_limit_bytes=38 * 2**20),
        cost_estimate=pl.CostEstimate(
            flops=4 * Y * half * cols * depth,
            bytes_accessed=2 * depth * (cols + 2 * Y * half),
            transcendentals=0,
        ),
        name="layer",
    )(place, factor, *blocks, tokens)


def half_kernel(place_ref, tokens_ref, half_ref, held, sems):
    pieces, rows, _ = held.shape
    start = place_ref[0] * (pieces * rows)
    loads, stores = [], []
    for n in range(pieces):
        here = pl.ds(pl.multiple_of(start + n * rows, 16), rows)
        loads.append(pltpu.make_async_copy(tokens_ref.at[here], held.at[n], sems.at[0, n]))
        there = pl.ds(n * rows, rows)
        stores.append(pltpu.make_async_copy(held.at[n], half_ref.at[there], sems.at[1, n]))
    for load in loads:
        load.start()
    for load, store in zip(loads, stores):
        load.wait()
        store.start()
    for store in stores:
        store.wait()


def core_half(tokens, c):
    rows, depth = tokens.shape
    pieces = 3
    anywhere = pl.BlockSpec(memory_space=pl.ANY)
    return pl.pallas_call(
        half_kernel,
        out_shape=jax.ShapeDtypeStruct((rows // 2, depth), tokens.dtype),
        in_specs=[pl.BlockSpec(memory_space=pltpu.SMEM), anywhere],
        out_specs=anywhere,
        scratch_shapes=[
            pltpu.VMEM((pieces, rows // 2 // pieces, depth), tokens.dtype),
            pltpu.SemaphoreType.DMA((2, pieces)),
        ],
        name="core_half",
    )(jnp.reshape(c, (1,)).astype(jnp.int32), tokens)


def tie(value, *after):
    return lax.optimization_barrier((value,) + after)[0]


class Chain:
    def __init__(self, block):
        self.ups, self.downs = [block], [block]

    def step(self):
        s = len(self.ups)
        up, down = self.ups[-1], self.downs[-1]
        if s > 2:
            up, down = tie(up, self.downs[-2]), tie(down, self.ups[-2])
        self.ups.append(lax.ppermute(up, "zl", [(z, z + 1) for z in range(s - 1, ZL - 1)]))
        self.downs.append(lax.ppermute(down, "zl", [(z, z - 1) for z in range(1, ZL + 1 - s)]))

    def after(self, *values):
        self.ups[-1] = tie(self.ups[-1], *values)
        self.downs[-1] = tie(self.downs[-1], *values)

    def blocks(self):
        return self.ups + self.downs[1:]


def weight_quarters(gate_weight, up_weight):
    depth, cols = gate_weight.shape
    return jnp.concatenate(
        [w.T.reshape(Y, cols // Y, depth) for w in (gate_weight, up_weight)], axis=1
    )


def out_partial(out_grad, out_factor):
    half = out_grad.shape[0] // 2
    grads = jnp.pad(out_grad.reshape(2, half, -1), ((0, 0), (0, 256 - half), (0, 0)))
    return lax.dot_general(
        out_factor, grads.reshape(512, -1), (((0,), (1,)), ((), ())),
        preferred_element_type=jnp.float32,
    )


def exchange_z(out, queries):
    rows, cols = queries.shape
    high = lax.reduce_precision(out, 8, 7)
    sent = jnp.concatenate(
        [v.astype(jnp.bfloat16) for v in (high, out - high)] + [queries.reshape(-1, out.shape[1])]
    )
    got = lax.all_gather(sent, "zh")
    count = out.shape[0]
    parts = got[:, : 2 * count].astype(jnp.float32)
    out = (parts[:, :count] + parts[:, count:]).sum(0)
    return out, got[:, 2 * count :].reshape(ZH, rows, cols)


def share_plane(out, queries):
    high = lax.reduce_precision(out, 8, 7)
    sent = jnp.concatenate(
        [v.astype(jnp.bfloat16) for v in (high, out - high)]
        + [queries.reshape(-1, out.shape[1])]
    )
    return share(sent, PLANE, Y * X * C)


def unpack_plane(got, count, rows, cols):
    lanes = got.shape[2]
    parts = got[:, : 2 * count].astype(jnp.float32)
    out = (parts[:, :count] + parts[:, count:]).reshape(Y, X * C * count, lanes)
    here = got.reshape((Y, X * C) + got.shape[1:])
    here = lax.dynamic_index_in_dim(here, lax.axis_index("y"), 0, keepdims=False)
    queries = here[:, 2 * count :].reshape(X, C, ZH, rows, cols)
    queries = queries.transpose(3, 0, 2, 1, 4).reshape(rows, -1)
    return out.transpose(1, 0, 2).reshape(X * C * count, Y * lanes), queries


def shards(tokens, gate_weight, up_weight, out_grad, in_factor, out_factor, queries):
    rows = tokens.shape[0]
    rank = in_factor.shape[1]
    half = rows // 2
    z, y, c = (lax.axis_index(name) for name in ("zl", "y", "c"))
    mine = core_half(tokens, c)
    plane_tokens = lax.all_gather(mine, ("y", "c"))
    quarter = in_factor.shape[0] // Y
    factor = lax.dynamic_slice_in_dim(in_factor, y * quarter, quarter, 0).T
    factor = jnp.pad(factor, ((0, 0), (0, 256 - quarter)))

    quarters = weight_quarters(gate_weight, up_weight)
    chain = Chain(lax.all_to_all(quarters, "y", 0, 0, tiled=True))
    out = out_partial(out_grad, out_factor)
    for s in range(1, ZL):
        chain.step()
        if s == 2:
            out = tie(out, chain.ups[-1], chain.downs[-1]).reshape(X * C, rank // (X * C), -1)
            out = lax.all_to_all(out, ("x", "c"), 0, 0, tiled=True).sum(0)
        if s == 4:
            chain.after(out)
            out = tie(out, chain.ups[-1], chain.downs[-1])
            out, query_rows = exchange_z(out, queries)
        if s == 6:
            chain.after(out, query_rows)
    out = tie(out, chain.ups[-1], chain.downs[-1])
    shared = share_plane(out, query_rows)

    place = jnp.stack([z]).astype(jnp.int32)
    in_part = layer(place, factor, chain.blocks(), plane_tokens)
    shared, in_part = lax.optimization_barrier((shared, in_part))
    out, query_rows = unpack_plane(shared, rank // (X * C), *queries.shape)
    in_proj = lax.all_to_all(in_part, PLANE, 0, 0, tiled=True)
    in_proj = in_proj.sum(0)

    seqs = Y * rows // LEN
    lane = jnp.arange(in_proj.shape[1])
    token = lane // 256 * half + lane % 256
    mask = (token // LEN)[None, :] == jnp.arange(seqs)[:, None]
    spread = jnp.where(mask[:, None, :], in_proj[None], 0.0).reshape(2 * seqs, -1)
    fragment = jnp.dot(spread, out.T, precision=HIGHEST) / jnp.sqrt(jnp.float32(LEN))
    fragment = fragment.reshape(seqs, 2 * rank)
    columns = share(fragment, ("zh", "zl"), ZH * ZL)
    columns = columns.reshape(ZH, ZL * seqs, 2 * rank).sum(0).astype(jnp.bfloat16)
    features = share(columns, PLANE, Y * X * C)
    return solve(features, query_rows)


def solution(mesh):
    fine = Mesh(mesh.devices.reshape(ZL, Y, X, ZH, C), ("zl", "y", "x", "zh", "c"))
    dp, tensor = ("zl", "y"), ("x", "zh", "c")
    in_specs = (
        P(dp, None),
        P(dp, tensor),
        P(dp, tensor),
        P(dp, tensor),
        P(tensor, None),
        P(tensor, None),
        P(dp, tensor),
    )
    return jax.shard_map(
        shards, mesh=fine, in_specs=in_specs, out_specs=P(dp, None), check_vma=False
    )
```

```python
import functools

import jax
import jax.numpy as jnp
from jax import lax
from jax.experimental import pallas as pl
from jax.experimental.pallas import tpu as pltpu
from jax.sharding import Mesh, PartitionSpec as P

LEN = 160
DAMPING = 0.1
ZL, Y, X, ZH, C = 8, 4, 4, 2, 2
PLANE = ("y", "x", "c")
HIGHEST = lax.Precision.HIGHEST


def solve_body(features_ref, queries_ref, out_ref):
    blocks, count, width = features_ref.shape
    total = blocks * width
    features = jnp.concatenate([features_ref[d] for d in range(blocks)], axis=1)
    both = jnp.concatenate([features, queries_ref[...]], axis=0)
    system = lax.dot_general(
        features, both, (((1,), (1,)), ((), ())), preferred_element_type=jnp.float32
    )
    row = lax.broadcasted_iota(jnp.int32, system.shape, 0)
    lane = lax.broadcasted_iota(jnp.int32, system.shape, 1)
    system = jnp.where(
        lane < count,
        system / total + jnp.where(row == lane, DAMPING, 0.0),
        system / (total**0.5),
    )
    on_diagonal = jnp.where(row == lane, system, 0.0)
    row_scale = lax.rsqrt(jnp.sum(on_diagonal, axis=1, keepdims=True))
    lane_scale = jnp.sum(jnp.where(row == lane, row_scale, 0.0), axis=0, keepdims=True)
    system = system * row_scale * jnp.where(lane < count, lane_scale, 1.0)
    groups = [system[8 * g : 8 * g + 8] for g in range(count // 8)]
    inner = lax.broadcasted_iota(jnp.int32, groups[0].shape, 0)
    whole = groups[0].shape
    side = 4
    for low in range(0, len(groups), side):
        inside = groups[low : low + side]
        for k in range(8 * low, 8 * (low + side), 2):
            g, r = k // 8 - low, k % 8
            p = jnp.broadcast_to(inside[g][r : r + 1], whole)
            q = jnp.broadcast_to(inside[g][r + 1 : r + 2], whole)
            a, b, c, d = (
                jnp.broadcast_to(v[:, n : n + 1], whole) for v in (p, q) for n in (k, k + 1)
            )
            inverse = 1.0 / (a * d - b * c)
            first = (d * inverse) * p - (b * inverse) * q
            second = (a * inverse) * q - (c * inverse) * p
            updated = [
                block
                - jnp.broadcast_to(block[:, k : k + 1], whole) * first
                - jnp.broadcast_to(block[:, k + 1 : k + 2], whole) * second
                for block in inside
            ]
            updated[g] = jnp.where(
                inner == r, first, jnp.where(inner == r + 1, second, updated[g])
            )
            inside = updated
        rest = jnp.concatenate(groups[:low] + groups[low + side :], axis=0)
        rest = rest - lax.dot_general(
            rest[:, 8 * low : 8 * (low + side)], jnp.concatenate(inside, axis=0),
            (((1,), (0,)), ((), ())),
            precision=HIGHEST, preferred_element_type=jnp.float32,
        )
        rest = [rest[8 * n : 8 * n + 8] for n in range(len(groups) - side)]
        groups = rest[:low] + inside + rest[low:]
    groups = [block * row_scale[8 * g : 8 * g + 8] for g, block in enumerate(groups)]
    width = system.shape[1]
    groups += [jnp.zeros_like(groups[0])] * (width // 8 - len(groups))
    solved = jnp.concatenate(groups, axis=0).T
    out_ref[...] = solved[count:, :count]


def solve(features, queries):
    count = features.shape[1]
    return pl.pallas_call(
        solve_body,
        out_shape=jax.ShapeDtypeStruct((queries.shape[0], count), jnp.float32),
        compiler_params=pltpu.CompilerParams(vmem_limit_bytes=32 * 2**20),
        name="solve",
    )(features, queries)


def share(x, axes, count):
    return lax.all_to_all(
        jnp.broadcast_to(x[None], (count,) + x.shape), axes, 0, 0, tiled=True
    )


def layer_kernel(place_ref, factor_ref, *refs):
    chains = 2 * ZL - 1
    blocks = refs[:chains]
    all_tokens, out_ref, weights, tokens, token_sems = refs[chains:]
    z = place_ref[0]
    hidden = blocks[0].shape[1] // 2
    half = all_tokens.shape[1]

    def token_copies(p):
        for c in range(2):
            yield pltpu.make_async_copy(
                all_tokens.at[2 * p + c], tokens.at[p, pl.ds(c * half, half)], token_sems.at[p, c]
            )

    for p in range(Y):
        for copy in token_copies(p):
            copy.start()

    gap = jnp.zeros((256 - hidden, 128), jnp.bfloat16)

    def place_block(at, owner):
        for k in range(Y):
            block = blocks[at][k]
            wide = jnp.concatenate([block[:hidden], gap, block[hidden:], gap], axis=0)
            weights[pl.ds(pl.multiple_of((owner * Y + k) * 128, 128), 128), :] = wide.T

    place_block(0, z)
    for s in range(1, ZL):
        @pl.when(z >= s)
        def _():
            place_block(s, z - s)

        @pl.when(z + s < ZL)
        def _():
            place_block(s + ZL - 1, z + s)

    def part(p, carry):
        for copy in token_copies(p):
            copy.wait()
        both = jnp.dot(tokens[p], weights[...], preferred_element_type=jnp.float32)
        gate, up = both[:, :256], both[:, 256:]
        value = (gate / (1.0 + jnp.exp(-gate)) * up).astype(jnp.bfloat16)
        proj = lax.dot_general(
            factor_ref[...], value, (((1,), (1,)), ((), ())),
            preferred_element_type=jnp.float32,
        )
        space = jnp.zeros((proj.shape[0], 256 - half), jnp.float32)
        proj = jnp.concatenate([proj[:, :half], space, proj[:, half:], space], axis=1)
        lanes = pl.ds(pl.multiple_of(p * 512, 512), 512)
        for d in range(out_ref.shape[0]):
            out_ref[d, :, lanes] = proj[2 * d : 2 * d + 2]
        return carry

    lax.fori_loop(0, Y, part, 0)


def layer(place, factor, blocks, tokens):
    _, half, depth = tokens.shape
    cols = blocks[0].shape[1]
    rank = factor.shape[0]
    vmem = pl.BlockSpec(memory_space=pltpu.VMEM)
    return pl.pallas_call(
        layer_kernel,
        out_shape=jax.ShapeDtypeStruct((rank // 2, 2, Y * 512), jnp.float32),
        in_specs=[pl.BlockSpec(memory_space=pltpu.SMEM)]
        + [vmem] * (1 + len(blocks))
        + [pl.BlockSpec(memory_space=pl.ANY)],
        out_specs=vmem,
        scratch_shapes=[
            pltpu.VMEM((depth, 512), jnp.bfloat16),
            pltpu.VMEM((Y, 2 * half, depth), jnp.bfloat16),
            pltpu.SemaphoreType.DMA((Y, 2)),
        ],
        compiler_params=pltpu.CompilerParams(vmem_limit_bytes=38 * 2**20),
        cost_estimate=pl.CostEstimate(
            flops=4 * Y * half * cols * depth,
            bytes_accessed=2 * depth * (cols + 2 * Y * half),
            transcendentals=0,
        ),
        name="layer",
    )(place, factor, *blocks, tokens)


def tie(value, *after):
    return lax.optimization_barrier((value,) + after)[0]


class Chain:
    def __init__(self, block):
        self.ups, self.downs = [block], [block]

    def step(self):
        s = len(self.ups)
        up, down = self.ups[-1], self.downs[-1]
        if s > 2:
            up, down = tie(up, self.downs[-2]), tie(down, self.ups[-2])
        self.ups.append(lax.ppermute(up, "zl", [(z, z + 1) for z in range(s - 1, ZL - 1)]))
        self.downs.append(lax.ppermute(down, "zl", [(z, z - 1) for z in range(1, ZL + 1 - s)]))

    def after(self, *values):
        self.ups[-1] = tie(self.ups[-1], *values)
        self.downs[-1] = tie(self.downs[-1], *values)

    def blocks(self):
        return self.ups + self.downs[1:]


def weight_quarters(gate_weight, up_weight):
    depth, cols = gate_weight.shape
    return jnp.concatenate(
        [w.T.reshape(Y, cols // Y, depth) for w in (gate_weight, up_weight)], axis=1
    )


def out_partial(out_grad, out_factor):
    half = out_grad.shape[0] // 2
    grads = jnp.pad(out_grad.reshape(2, half, -1), ((0, 0), (0, 256 - half), (0, 0)))
    return lax.dot_general(
        out_factor, grads.reshape(512, -1), (((0,), (1,)), ((), ())),
        preferred_element_type=jnp.float32,
    )


def exchange_z(out, queries):
    rows, cols = queries.shape
    high = lax.reduce_precision(out, 8, 7)
    sent = jnp.concatenate(
        [v.astype(jnp.bfloat16) for v in (high, out - high)] + [queries.reshape(-1, out.shape[1])]
    )
    got = lax.all_gather(sent, "zh")
    count = out.shape[0]
    parts = got[:, : 2 * count].astype(jnp.float32)
    out = (parts[:, :count] + parts[:, count:]).sum(0)
    return out, got[:, 2 * count :].reshape(ZH, rows, cols)


def share_queries(queries):
    _, rows, cols = queries.shape
    got = share(queries, ("x", "c"), X * C).reshape(X, C, ZH, rows, cols)
    return got.transpose(3, 0, 2, 1, 4).reshape(rows, -1)


def shards(tokens, gate_weight, up_weight, out_grad, in_factor, out_factor, queries):
    rows = tokens.shape[0]
    rank = in_factor.shape[1]
    half = rows // 2
    z, y, c = (lax.axis_index(name) for name in ("zl", "y", "c"))
    mine = lax.dynamic_slice_in_dim(tokens, c * half, half, 0)
    plane_tokens = lax.all_gather(mine, ("y", "c"))
    quarter = in_factor.shape[0] // Y
    factor = lax.dynamic_slice_in_dim(in_factor, y * quarter, quarter, 0).T
    factor = jnp.pad(factor, ((0, 0), (0, 256 - quarter)))

    quarters = weight_quarters(gate_weight, up_weight)
    chain = Chain(lax.all_to_all(quarters, "y", 0, 0, tiled=True))
    out = out_partial(out_grad, out_factor).reshape(X * C, rank // (X * C), -1)
    for s in range(1, ZL):
        chain.step()
        if s == 1:
            out = tie(out, chain.ups[-1])
            out = lax.all_to_all(out, ("x", "c"), 0, 0, tiled=True).sum(0)
        if s == 5:
            chain.after(out)
            out = tie(out, chain.ups[-1])
            out, query_rows = exchange_z(out, queries)
        if s == 6:
            chain.after(out, plane_tokens)
            out = tie(out, chain.ups[-1])
            out = share(out, PLANE, Y * X * C)
    out = out.reshape(Y, rank, -1).transpose(1, 0, 2).reshape(rank, -1)

    place = jnp.stack([z]).astype(jnp.int32)
    in_part = layer(place, factor, chain.blocks(), plane_tokens)
    in_proj = lax.all_to_all(in_part, PLANE, 0, 0, tiled=True)
    in_proj = in_proj.sum(0)

    seqs = Y * rows // LEN
    lane = jnp.arange(in_proj.shape[1])
    token = lane // 256 * half + lane % 256
    mask = (token // LEN)[None, :] == jnp.arange(seqs)[:, None]
    spread = jnp.where(mask[:, None, :], in_proj[None], 0.0).reshape(2 * seqs, -1)
    fragment = jnp.dot(spread, out.T, precision=HIGHEST) / jnp.sqrt(jnp.float32(LEN))
    fragment = fragment.reshape(seqs, 2 * rank)
    fragment, query_rows = lax.optimization_barrier((fragment, query_rows))
    columns = share(fragment, ("zh", "zl"), ZH * ZL)
    query_rows = share_queries(query_rows)
    columns, query_rows = lax.optimization_barrier((columns, query_rows))
    columns = columns.reshape(ZH, ZL * seqs, 2 * rank).sum(0).astype(jnp.bfloat16)
    features = share(columns, PLANE, Y * X * C)
    return solve(features, query_rows)


def solution(mesh):
    fine = Mesh(mesh.devices.reshape(ZL, Y, X, ZH, C), ("zl", "y", "x", "zh", "c"))
    dp, tensor = ("zl", "y"), ("x", "zh", "c")
    in_specs = (
        P(dp, None),
        P(dp, tensor),
        P(dp, tensor),
        P(dp, tensor),
        P(tensor, None),
        P(tensor, None),
        P(dp, tensor),
    )
    return jax.shard_map(
        shards, mesh=fine, in_specs=in_specs, out_specs=P(dp, None), check_vma=False
    )
```

```python
import functools

import jax
import jax.numpy as jnp
from jax import lax
from jax.experimental import pallas as pl
from jax.experimental.pallas import tpu as pltpu
from jax.sharding import Mesh, PartitionSpec as P

LEN = 160
DAMPING = 0.1
ZL, Y, X, ZH, C = 8, 4, 4, 2, 2
PLANE = ("y", "x", "c")
HIGHEST = lax.Precision.HIGHEST


def solve_body(features_ref, queries_ref, out_ref):
    blocks, count, width = features_ref.shape
    total = blocks * width
    features = jnp.concatenate([features_ref[d] for d in range(blocks)], axis=1)
    both = jnp.concatenate([features, queries_ref[...]], axis=0)
    system = lax.dot_general(
        features, both, (((1,), (1,)), ((), ())), preferred_element_type=jnp.float32
    )
    row = lax.broadcasted_iota(jnp.int32, system.shape, 0)
    lane = lax.broadcasted_iota(jnp.int32, system.shape, 1)
    system = jnp.where(
        lane < count,
        system / total + jnp.where(row == lane, DAMPING, 0.0),
        system / (total**0.5),
    )
    on_diagonal = jnp.where(row == lane, system, 0.0)
    row_scale = lax.rsqrt(jnp.sum(on_diagonal, axis=1, keepdims=True))
    lane_scale = jnp.sum(jnp.where(row == lane, row_scale, 0.0), axis=0, keepdims=True)
    system = system * row_scale * jnp.where(lane < count, lane_scale, 1.0)
    groups = [system[8 * g : 8 * g + 8] for g in range(count // 8)]
    inner = lax.broadcasted_iota(jnp.int32, groups[0].shape, 0)
    whole = groups[0].shape
    side = 4
    for low in range(0, len(groups), side):
        inside = groups[low : low + side]
        for k in range(8 * low, 8 * (low + side), 2):
            g, r = k // 8 - low, k % 8
            p = jnp.broadcast_to(inside[g][r : r + 1], whole)
            q = jnp.broadcast_to(inside[g][r + 1 : r + 2], whole)
            a, b, c, d = (
                jnp.broadcast_to(v[:, n : n + 1], whole) for v in (p, q) for n in (k, k + 1)
            )
            inverse = 1.0 / (a * d - b * c)
            first = (d * inverse) * p - (b * inverse) * q
            second = (a * inverse) * q - (c * inverse) * p
            updated = [
                block
                - jnp.broadcast_to(block[:, k : k + 1], whole) * first
                - jnp.broadcast_to(block[:, k + 1 : k + 2], whole) * second
                for block in inside
            ]
            updated[g] = jnp.where(
                inner == r, first, jnp.where(inner == r + 1, second, updated[g])
            )
            inside = updated
        rest = jnp.concatenate(groups[:low] + groups[low + side :], axis=0)
        rest = rest - lax.dot_general(
            rest[:, 8 * low : 8 * (low + side)], jnp.concatenate(inside, axis=0),
            (((1,), (0,)), ((), ())),
            precision=HIGHEST, preferred_element_type=jnp.float32,
        )
        rest = [rest[8 * n : 8 * n + 8] for n in range(len(groups) - side)]
        groups = rest[:low] + inside + rest[low:]
    groups = [block * row_scale[8 * g : 8 * g + 8] for g, block in enumerate(groups)]
    width = system.shape[1]
    groups += [jnp.zeros_like(groups[0])] * (width // 8 - len(groups))
    solved = jnp.concatenate(groups, axis=0).T
    out_ref[...] = solved[count:, :count]


def solve(features, queries):
    count = features.shape[1]
    return pl.pallas_call(
        solve_body,
        out_shape=jax.ShapeDtypeStruct((queries.shape[0], count), jnp.float32),
        compiler_params=pltpu.CompilerParams(vmem_limit_bytes=32 * 2**20),
        name="solve",
    )(features, queries)


def share(x, axes, count):
    return lax.all_to_all(
        jnp.broadcast_to(x[None], (count,) + x.shape), axes, 0, 0, tiled=True
    )


def layer_kernel(place_ref, factor_ref, *refs):
    chains = 2 * ZL - 1
    blocks = refs[:chains]
    all_tokens, out_ref, weights, tokens, token_sems = refs[chains:]
    z = place_ref[0]
    hidden = blocks[0].shape[1] // 2
    half = all_tokens.shape[1]

    def token_copies(p):
        for c in range(2):
            yield pltpu.make_async_copy(
                all_tokens.at[2 * p + c], tokens.at[p, pl.ds(c * half, half)], token_sems.at[p, c]
            )

    for p in range(Y):
        for copy in token_copies(p):
            copy.start()

    gap = jnp.zeros((256 - hidden, 128), jnp.bfloat16)

    def place_block(at, owner):
        for k in range(Y):
            block = blocks[at][k]
            wide = jnp.concatenate([block[:hidden], gap, block[hidden:], gap], axis=0)
            weights[pl.ds(pl.multiple_of((owner * Y + k) * 128, 128), 128), :] = wide.T

    place_block(0, z)
    for s in range(1, ZL):
        @pl.when(z >= s)
        def _():
            place_block(s, z - s)

        @pl.when(z + s < ZL)
        def _():
            place_block(s + ZL - 1, z + s)

    def part(p, carry):
        for copy in token_copies(p):
            copy.wait()
        both = jnp.dot(tokens[p], weights[...], preferred_element_type=jnp.float32)
        gate, up = both[:, :256], both[:, 256:]
        value = (gate / (1.0 + jnp.exp(-gate)) * up).astype(jnp.bfloat16)
        proj = lax.dot_general(
            factor_ref[...], value, (((1,), (1,)), ((), ())),
            preferred_element_type=jnp.float32,
        )
        space = jnp.zeros((proj.shape[0], 256 - half), jnp.float32)
        proj = jnp.concatenate([proj[:, :half], space, proj[:, half:], space], axis=1)
        lanes = pl.ds(pl.multiple_of(p * 512, 512), 512)
        for d in range(out_ref.shape[0]):
            out_ref[d, :, lanes] = proj[2 * d : 2 * d + 2]
        return carry

    lax.fori_loop(0, Y, part, 0)


def layer(place, factor, blocks, tokens):
    _, half, depth = tokens.shape
    cols = blocks[0].shape[1]
    rank = factor.shape[0]
    vmem = pl.BlockSpec(memory_space=pltpu.VMEM)
    return pl.pallas_call(
        layer_kernel,
        out_shape=jax.ShapeDtypeStruct((rank // 2, 2, Y * 512), jnp.float32),
        in_specs=[pl.BlockSpec(memory_space=pltpu.SMEM)]
        + [vmem] * (1 + len(blocks))
        + [pl.BlockSpec(memory_space=pl.ANY)],
        out_specs=vmem,
        scratch_shapes=[
            pltpu.VMEM((depth, 512), jnp.bfloat16),
            pltpu.VMEM((Y, 2 * half, depth), jnp.bfloat16),
            pltpu.SemaphoreType.DMA((Y, 2)),
        ],
        compiler_params=pltpu.CompilerParams(vmem_limit_bytes=38 * 2**20),
        cost_estimate=pl.CostEstimate(
            flops=4 * Y * half * cols * depth,
            bytes_accessed=2 * depth * (cols + 2 * Y * half),
            transcendentals=0,
        ),
        name="layer",
    )(place, factor, *blocks, tokens)


def tie(value, *after):
    return lax.optimization_barrier((value,) + after)[0]


class Chain:
    def __init__(self, block):
        self.ups, self.downs = [block], [block]

    def step(self):
        s = len(self.ups)
        up, down = self.ups[-1], self.downs[-1]
        if s > 2:
            up, down = tie(up, self.downs[-2]), tie(down, self.ups[-2])
        self.ups.append(lax.ppermute(up, "zl", [(z, z + 1) for z in range(s - 1, ZL - 1)]))
        self.downs.append(lax.ppermute(down, "zl", [(z, z - 1) for z in range(1, ZL + 1 - s)]))

    def join(self, value):
        self.ups[-1], self.downs[-1], value = lax.optimization_barrier(
            (self.ups[-1], self.downs[-1], value)
        )
        return value

    def blocks(self):
        return self.ups + self.downs[1:]


def weight_quarters(gate_weight, up_weight):
    depth, cols = gate_weight.shape
    return jnp.concatenate(
        [w.T.reshape(Y, cols // Y, depth) for w in (gate_weight, up_weight)], axis=1
    )


def out_partial(out_grad, out_factor):
    half = out_grad.shape[0] // 2
    grads = jnp.pad(out_grad.reshape(2, half, -1), ((0, 0), (0, 256 - half), (0, 0)))
    return lax.dot_general(
        out_factor, grads.reshape(512, -1), (((0,), (1,)), ((), ())),
        preferred_element_type=jnp.float32,
    )


def exchange_z(out, queries):
    rows, cols = queries.shape
    high = lax.reduce_precision(out, 8, 7)
    sent = jnp.concatenate(
        [v.astype(jnp.bfloat16) for v in (high, out - high)] + [queries.reshape(-1, out.shape[1])]
    )
    got = lax.all_gather(sent, "zh")
    count = out.shape[0]
    parts = got[:, : 2 * count].astype(jnp.float32)
    out = (parts[:, :count] + parts[:, count:]).sum(0)
    return out, got[:, 2 * count :].reshape(ZH, rows, cols)


def share_plane(out, queries):
    high = lax.reduce_precision(out, 8, 7)
    sent = jnp.concatenate(
        [v.astype(jnp.bfloat16) for v in (high, out - high)]
        + [queries.reshape(-1, out.shape[1])]
    )
    return lax.all_gather(sent, PLANE)


def unpack_plane(got, count, rows, cols):
    lanes = got.shape[2]
    parts = got[:, : 2 * count].astype(jnp.float32)
    out = (parts[:, :count] + parts[:, count:]).reshape(Y, X * C * count, lanes)
    here = got.reshape((Y, X * C) + got.shape[1:])
    here = lax.dynamic_index_in_dim(here, lax.axis_index("y"), 0, keepdims=False)
    queries = here[:, 2 * count :].reshape(X, C, ZH, rows, cols)
    queries = queries.transpose(3, 0, 2, 1, 4).reshape(rows, -1)
    return out.transpose(1, 0, 2).reshape(X * C * count, Y * lanes), queries


def shards(tokens, gate_weight, up_weight, out_grad, in_factor, out_factor, queries):
    rows = tokens.shape[0]
    rank = in_factor.shape[1]
    half = rows // 2
    z, y, c = (lax.axis_index(name) for name in ("zl", "y", "c"))
    mine = lax.dynamic_slice_in_dim(tokens, c * half, half, 0)
    plane_tokens = lax.all_gather(mine, ("y", "c"))
    quarter = in_factor.shape[0] // Y
    factor = lax.dynamic_slice_in_dim(in_factor, y * quarter, quarter, 0).T
    factor = jnp.pad(factor, ((0, 0), (0, 256 - quarter)))

    quarters = weight_quarters(gate_weight, up_weight)
    chain = Chain(lax.all_to_all(quarters, "y", 0, 0, tiled=True))
    out = out_partial(out_grad, out_factor).reshape(X * C, rank // (X * C), -1)
    for s in range(1, ZL):
        chain.step()
        if s == 2:
            out = lax.all_to_all(out, ("x", "c"), 0, 0, tiled=True).sum(0)
        if s == 4:
            out = exchange_z(out, queries)
        if s < 5:
            out = chain.join(out)
        if s == 6:
            plane_tokens = chain.join(plane_tokens)
    out, query_rows = out
    shared = share_plane(out, query_rows)

    place = jnp.stack([z]).astype(jnp.int32)
    in_part = layer(place, factor, chain.blocks(), plane_tokens)
    in_proj = lax.all_to_all(in_part, PLANE, 0, 0, tiled=True)
    in_proj, shared = lax.optimization_barrier((in_proj, shared))
    out, query_rows = unpack_plane(shared, rank // (X * C), *queries.shape)
    in_proj = in_proj.sum(0)

    seqs = Y * rows // LEN
    lane = jnp.arange(in_proj.shape[1])
    token = lane // 256 * half + lane % 256
    mask = (token // LEN)[None, :] == jnp.arange(seqs)[:, None]
    spread = jnp.where(mask[:, None, :], in_proj[None], 0.0).reshape(2 * seqs, -1)
    fragment = jnp.dot(spread, out.T, precision=HIGHEST) / jnp.sqrt(jnp.float32(LEN))
    fragment = fragment.reshape(seqs, 2 * rank)
    columns = share(fragment, ("zh", "zl"), ZH * ZL)
    columns = columns.reshape(ZH, ZL * seqs, 2 * rank).sum(0).astype(jnp.bfloat16)
    features = share(columns, PLANE, Y * X * C)
    return solve(features, query_rows)


def solution(mesh):
    fine = Mesh(mesh.devices.reshape(ZL, Y, X, ZH, C), ("zl", "y", "x", "zh", "c"))
    dp, tensor = ("zl", "y"), ("x", "zh", "c")
    in_specs = (
        P(dp, None),
        P(dp, tensor),
        P(dp, tensor),
        P(dp, tensor),
        P(tensor, None),
        P(tensor, None),
        P(dp, tensor),
    )
    return jax.shard_map(
        shards, mesh=fine, in_specs=in_specs, out_specs=P(dp, None), check_vma=False
    )
```

```python
import functools

import jax
import jax.numpy as jnp
from jax import lax
from jax.experimental import pallas as pl
from jax.experimental.pallas import tpu as pltpu
from jax.sharding import Mesh, PartitionSpec as P

LEN = 160
DAMPING = 0.1
ZL, Y, X, ZH, C = 8, 4, 4, 2, 2
PLANE = ("y", "x", "c")
HIGHEST = lax.Precision.HIGHEST


def solve_body(features_ref, queries_ref, out_ref):
    blocks, count, width = features_ref.shape
    total = blocks * width
    features = jnp.concatenate([features_ref[d] for d in range(blocks)], axis=1)
    both = jnp.concatenate([features, queries_ref[...]], axis=0)
    system = lax.dot_general(
        features, both, (((1,), (1,)), ((), ())), preferred_element_type=jnp.float32
    )
    row = lax.broadcasted_iota(jnp.int32, system.shape, 0)
    lane = lax.broadcasted_iota(jnp.int32, system.shape, 1)
    system = jnp.where(
        lane < count,
        system / total + jnp.where(row == lane, DAMPING, 0.0),
        system / (total**0.5),
    )
    on_diagonal = jnp.where(row == lane, system, 0.0)
    row_scale = lax.rsqrt(jnp.sum(on_diagonal, axis=1, keepdims=True))
    lane_scale = jnp.sum(jnp.where(row == lane, row_scale, 0.0), axis=0, keepdims=True)
    system = system * row_scale * jnp.where(lane < count, lane_scale, 1.0)
    groups = [system[8 * g : 8 * g + 8] for g in range(count // 8)]
    inner = lax.broadcasted_iota(jnp.int32, groups[0].shape, 0)
    whole = groups[0].shape
    side = 4
    for low in range(0, len(groups), side):
        inside = groups[low : low + side]
        for k in range(8 * low, 8 * (low + side), 2):
            g, r = k // 8 - low, k % 8
            p = jnp.broadcast_to(inside[g][r : r + 1], whole)
            q = jnp.broadcast_to(inside[g][r + 1 : r + 2], whole)
            a, b, c, d = (
                jnp.broadcast_to(v[:, n : n + 1], whole) for v in (p, q) for n in (k, k + 1)
            )
            inverse = 1.0 / (a * d - b * c)
            first = (d * inverse) * p - (b * inverse) * q
            second = (a * inverse) * q - (c * inverse) * p
            updated = [
                block
                - jnp.broadcast_to(block[:, k : k + 1], whole) * first
                - jnp.broadcast_to(block[:, k + 1 : k + 2], whole) * second
                for block in inside
            ]
            updated[g] = jnp.where(
                inner == r, first, jnp.where(inner == r + 1, second, updated[g])
            )
            inside = updated
        rest = jnp.concatenate(groups[:low] + groups[low + side :], axis=0)
        rest = rest - lax.dot_general(
            rest[:, 8 * low : 8 * (low + side)], jnp.concatenate(inside, axis=0),
            (((1,), (0,)), ((), ())),
            precision=HIGHEST, preferred_element_type=jnp.float32,
        )
        rest = [rest[8 * n : 8 * n + 8] for n in range(len(groups) - side)]
        groups = rest[:low] + inside + rest[low:]
    groups = [block * row_scale[8 * g : 8 * g + 8] for g, block in enumerate(groups)]
    width = system.shape[1]
    groups += [jnp.zeros_like(groups[0])] * (width // 8 - len(groups))
    solved = jnp.concatenate(groups, axis=0).T
    out_ref[...] = solved[count:, :count]


def solve(features, queries):
    count = features.shape[1]
    return pl.pallas_call(
        solve_body,
        out_shape=jax.ShapeDtypeStruct((queries.shape[0], count), jnp.float32),
        compiler_params=pltpu.CompilerParams(vmem_limit_bytes=32 * 2**20),
        name="solve",
    )(features, queries)


def share(x, axes, count):
    return lax.all_to_all(
        jnp.broadcast_to(x[None], (count,) + x.shape), axes, 0, 0, tiled=True
    )


def layer_kernel(place_ref, factor_ref, *refs):
    chains = 2 * ZL - 1
    blocks = refs[:chains]
    all_tokens, out_ref, weights, tokens, token_sems = refs[chains:]
    z = place_ref[0]
    hidden = blocks[0].shape[1] // 2
    half = all_tokens.shape[1]

    def token_copies(p):
        for c in range(2):
            yield pltpu.make_async_copy(
                all_tokens.at[2 * p + c], tokens.at[p, pl.ds(c * half, half)], token_sems.at[p, c]
            )

    for p in range(Y):
        for copy in token_copies(p):
            copy.start()

    gap = jnp.zeros((256 - hidden, 128), jnp.bfloat16)

    def place_block(at, owner):
        for k in range(Y):
            block = blocks[at][k]
            wide = jnp.concatenate([block[:hidden], gap, block[hidden:], gap], axis=0)
            weights[pl.ds(pl.multiple_of((owner * Y + k) * 128, 128), 128), :] = wide.T

    place_block(0, z)
    for s in range(1, ZL):
        @pl.when(z >= s)
        def _():
            place_block(s, z - s)

        @pl.when(z + s < ZL)
        def _():
            place_block(s + ZL - 1, z + s)

    def part(p, carry):
        for copy in token_copies(p):
            copy.wait()
        both = jnp.dot(tokens[p], weights[...], preferred_element_type=jnp.float32)
        gate, up = both[:, :256], both[:, 256:]
        value = (gate / (1.0 + jnp.exp(-gate)) * up).astype(jnp.bfloat16)
        proj = lax.dot_general(
            factor_ref[...], value, (((1,), (1,)), ((), ())),
            preferred_element_type=jnp.float32,
        )
        space = jnp.zeros((proj.shape[0], 256 - half), jnp.float32)
        proj = jnp.concatenate([proj[:, :half], space, proj[:, half:], space], axis=1)
        lanes = pl.ds(pl.multiple_of(p * 512, 512), 512)
        for d in range(out_ref.shape[0]):
            out_ref[d, :, lanes] = proj[2 * d : 2 * d + 2]
        return carry

    lax.fori_loop(0, Y, part, 0)


def layer(place, factor, blocks, tokens):
    _, half, depth = tokens.shape
    cols = blocks[0].shape[1]
    rank = factor.shape[0]
    vmem = pl.BlockSpec(memory_space=pltpu.VMEM)
    return pl.pallas_call(
        layer_kernel,
        out_shape=jax.ShapeDtypeStruct((rank // 2, 2, Y * 512), jnp.float32),
        in_specs=[pl.BlockSpec(memory_space=pltpu.SMEM)]
        + [vmem] * (1 + len(blocks))
        + [pl.BlockSpec(memory_space=pl.ANY)],
        out_specs=vmem,
        scratch_shapes=[
            pltpu.VMEM((depth, 512), jnp.bfloat16),
            pltpu.VMEM((Y, 2 * half, depth), jnp.bfloat16),
            pltpu.SemaphoreType.DMA((Y, 2)),
        ],
        compiler_params=pltpu.CompilerParams(vmem_limit_bytes=38 * 2**20),
        cost_estimate=pl.CostEstimate(
            flops=4 * Y * half * cols * depth,
            bytes_accessed=2 * depth * (cols + 2 * Y * half),
            transcendentals=0,
        ),
        name="layer",
    )(place, factor, *blocks, tokens)


def tie(value, *after):
    return lax.optimization_barrier((value,) + after)[0]


class Chain:
    def __init__(self, block):
        self.ups, self.downs = [block], [block]

    def step(self):
        s = len(self.ups)
        up, down = self.ups[-1], self.downs[-1]
        if s > 2:
            up, down = tie(up, self.downs[-2]), tie(down, self.ups[-2])
        self.ups.append(lax.ppermute(up, "zl", [(z, z + 1) for z in range(s - 1, ZL - 1)]))
        self.downs.append(lax.ppermute(down, "zl", [(z, z - 1) for z in range(1, ZL + 1 - s)]))

    def after(self, *values):
        self.ups[-1] = tie(self.ups[-1], *values)
        self.downs[-1] = tie(self.downs[-1], *values)

    def blocks(self):
        return self.ups + self.downs[1:]


def weight_quarters(gate_weight, up_weight):
    depth, cols = gate_weight.shape
    return jnp.concatenate(
        [w.T.reshape(Y, cols // Y, depth) for w in (gate_weight, up_weight)], axis=1
    )


def out_partial(out_grad, out_factor):
    half = out_grad.shape[0] // 2
    grads = jnp.pad(out_grad.reshape(2, half, -1), ((0, 0), (0, 256 - half), (0, 0)))
    return lax.dot_general(
        out_factor, grads.reshape(512, -1), (((0,), (1,)), ((), ())),
        preferred_element_type=jnp.float32,
    )


def exchange_z(out, queries):
    rows, cols = queries.shape
    high = lax.reduce_precision(out, 8, 7)
    sent = jnp.concatenate(
        [v.astype(jnp.bfloat16) for v in (high, out - high)] + [queries.reshape(-1, out.shape[1])]
    )
    got = lax.all_gather(sent, "zh")
    count = out.shape[0]
    parts = got[:, : 2 * count].astype(jnp.float32)
    out = (parts[:, :count] + parts[:, count:]).sum(0)
    return out, got[:, 2 * count :].reshape(ZH, rows, cols)


def share_plane(out, queries):
    high = lax.reduce_precision(out, 8, 7)
    sent = jnp.concatenate(
        [v.astype(jnp.bfloat16) for v in (high, out - high)]
        + [queries.reshape(-1, out.shape[1])]
    )
    return lax.all_gather(sent, PLANE)


def unpack_queries(got, first, rows, cols):
    here = got.reshape((Y, X * C) + got.shape[1:])
    here = lax.dynamic_index_in_dim(here, lax.axis_index("y"), 0, keepdims=False)
    queries = here[:, first:].reshape(X, C, ZH, rows, cols)
    return queries.transpose(3, 0, 2, 1, 4).reshape(rows, -1)


def shards(tokens, gate_weight, up_weight, out_grad, in_factor, out_factor, queries):
    rows = tokens.shape[0]
    rank = in_factor.shape[1]
    half = rows // 2
    z, y, c = (lax.axis_index(name) for name in ("zl", "y", "c"))
    mine = lax.dynamic_slice_in_dim(tokens, c * half, half, 0)
    plane_tokens = lax.all_gather(mine, ("y", "c"))
    quarter = in_factor.shape[0] // Y
    factor = lax.dynamic_slice_in_dim(in_factor, y * quarter, quarter, 0).T
    factor = jnp.pad(factor, ((0, 0), (0, 256 - quarter)))

    quarters = weight_quarters(gate_weight, up_weight)
    chain = Chain(lax.all_to_all(quarters, "y", 0, 0, tiled=True))
    out = out_partial(out_grad, out_factor).reshape(X * C, rank // (X * C), -1)
    for s in range(1, ZL):
        chain.step()
        if s == 1:
            out = tie(out, chain.ups[-1])
            out = lax.all_to_all(out, ("x", "c"), 0, 0, tiled=True).sum(0)
        if s == 5:
            chain.after(out)
            out = tie(out, chain.ups[-1])
            out, query_rows = exchange_z(out, queries)
        if s == 6:
            chain.after(out, plane_tokens)
    shared = share_plane(out, query_rows)
    out = tie(out, chain.ups[-1], chain.downs[-1])
    out = share(out, PLANE, Y * X * C)

    place = jnp.stack([z]).astype(jnp.int32)
    in_part = layer(place, factor, chain.blocks(), plane_tokens)
    in_part, out = lax.optimization_barrier((in_part, out))
    out = out.reshape(Y, rank, -1).transpose(1, 0, 2).reshape(rank, -1)
    in_proj = lax.all_to_all(in_part, PLANE, 0, 0, tiled=True)
    in_proj = in_proj.sum(0)

    seqs = Y * rows // LEN
    lane = jnp.arange(in_proj.shape[1])
    token = lane // 256 * half + lane % 256
    mask = (token // LEN)[None, :] == jnp.arange(seqs)[:, None]
    spread = jnp.where(mask[:, None, :], in_proj[None], 0.0).reshape(2 * seqs, -1)
    fragment = jnp.dot(spread, out.T, precision=HIGHEST) / jnp.sqrt(jnp.float32(LEN))
    fragment = fragment.reshape(seqs, 2 * rank)
    columns = share(fragment, ("zh", "zl"), ZH * ZL)
    columns, shared = lax.optimization_barrier((columns, shared))
    columns = columns.reshape(ZH, ZL * seqs, 2 * rank).sum(0).astype(jnp.bfloat16)
    query_rows = unpack_queries(shared, 2 * rank // (X * C), *queries.shape)
    features = share(columns, PLANE, Y * X * C)
    return solve(features, query_rows)


def solution(mesh):
    fine = Mesh(mesh.devices.reshape(ZL, Y, X, ZH, C), ("zl", "y", "x", "zh", "c"))
    dp, tensor = ("zl", "y"), ("x", "zh", "c")
    in_specs = (
        P(dp, None),
        P(dp, tensor),
        P(dp, tensor),
        P(dp, tensor),
        P(tensor, None),
        P(tensor, None),
        P(dp, tensor),
    )
    return jax.shard_map(
        shards, mesh=fine, in_specs=in_specs, out_specs=P(dp, None), check_vma=False
    )
```

```python
import functools

import jax
import jax.numpy as jnp
from jax import lax
from jax.experimental import pallas as pl
from jax.experimental.pallas import tpu as pltpu
from jax.sharding import Mesh, PartitionSpec as P

LEN = 160
DAMPING = 0.1
ZL, Y, X, ZH, C = 8, 4, 4, 2, 2
PLANE = ("y", "x", "c")
HIGHEST = lax.Precision.HIGHEST


def solve_body(features_ref, queries_ref, out_ref):
    blocks, count, width = features_ref.shape
    total = blocks * width
    features = jnp.concatenate([features_ref[d] for d in range(blocks)], axis=1)
    both = jnp.concatenate([features, queries_ref[...]], axis=0)
    system = lax.dot_general(
        features, both, (((1,), (1,)), ((), ())), preferred_element_type=jnp.float32
    )
    row = lax.broadcasted_iota(jnp.int32, system.shape, 0)
    lane = lax.broadcasted_iota(jnp.int32, system.shape, 1)
    system = jnp.where(
        lane < count,
        system / total + jnp.where(row == lane, DAMPING, 0.0),
        system / (total**0.5),
    )
    on_diagonal = jnp.where(row == lane, system, 0.0)
    row_scale = lax.rsqrt(jnp.sum(on_diagonal, axis=1, keepdims=True))
    lane_scale = jnp.sum(jnp.where(row == lane, row_scale, 0.0), axis=0, keepdims=True)
    system = system * row_scale * jnp.where(lane < count, lane_scale, 1.0)
    groups = [system[8 * g : 8 * g + 8] for g in range(count // 8)]
    inner = lax.broadcasted_iota(jnp.int32, groups[0].shape, 0)
    whole = groups[0].shape
    side = 4
    for low in range(0, len(groups), side):
        inside = groups[low : low + side]
        for k in range(8 * low, 8 * (low + side), 2):
            g, r = k // 8 - low, k % 8
            p = jnp.broadcast_to(inside[g][r : r + 1], whole)
            q = jnp.broadcast_to(inside[g][r + 1 : r + 2], whole)
            a, b, c, d = (
                jnp.broadcast_to(v[:, n : n + 1], whole) for v in (p, q) for n in (k, k + 1)
            )
            inverse = 1.0 / (a * d - b * c)
            first = (d * inverse) * p - (b * inverse) * q
            second = (a * inverse) * q - (c * inverse) * p
            updated = [
                block
                - jnp.broadcast_to(block[:, k : k + 1], whole) * first
                - jnp.broadcast_to(block[:, k + 1 : k + 2], whole) * second
                for block in inside
            ]
            updated[g] = jnp.where(
                inner == r, first, jnp.where(inner == r + 1, second, updated[g])
            )
            inside = updated
        rest = jnp.concatenate(groups[:low] + groups[low + side :], axis=0)
        rest = rest - lax.dot_general(
            rest[:, 8 * low : 8 * (low + side)], jnp.concatenate(inside, axis=0),
            (((1,), (0,)), ((), ())),
            precision=HIGHEST, preferred_element_type=jnp.float32,
        )
        rest = [rest[8 * n : 8 * n + 8] for n in range(len(groups) - side)]
        groups = rest[:low] + inside + rest[low:]
    groups = [block * row_scale[8 * g : 8 * g + 8] for g, block in enumerate(groups)]
    width = system.shape[1]
    groups += [jnp.zeros_like(groups[0])] * (width // 8 - len(groups))
    solved = jnp.concatenate(groups, axis=0).T
    out_ref[...] = solved[count:, :count]


def solve(features, queries):
    count = features.shape[1]
    return pl.pallas_call(
        solve_body,
        out_shape=jax.ShapeDtypeStruct((queries.shape[0], count), jnp.float32),
        compiler_params=pltpu.CompilerParams(vmem_limit_bytes=32 * 2**20),
        name="solve",
    )(features, queries)


def share(x, axes, count):
    return lax.all_to_all(
        jnp.broadcast_to(x[None], (count,) + x.shape), axes, 0, 0, tiled=True
    )


def layer_kernel(place_ref, factor_ref, *refs):
    chains = 2 * ZL - 1
    blocks = refs[:chains]
    all_tokens, out_ref, weights, tokens, token_sems = refs[chains:]
    z = place_ref[0]
    hidden = blocks[0].shape[1] // 2
    half = all_tokens.shape[1]

    def token_copies(p):
        for c in range(2):
            yield pltpu.make_async_copy(
                all_tokens.at[2 * p + c], tokens.at[p, pl.ds(c * half, half)], token_sems.at[p, c]
            )

    for p in range(Y):
        for copy in token_copies(p):
            copy.start()

    gap = jnp.zeros((256 - hidden, 128), jnp.bfloat16)

    def place_block(at, owner):
        for k in range(Y):
            block = blocks[at][k]
            wide = jnp.concatenate([block[:hidden], gap, block[hidden:], gap], axis=0)
            weights[pl.ds(pl.multiple_of((owner * Y + k) * 128, 128), 128), :] = wide.T

    place_block(0, z)
    for s in range(1, ZL):
        @pl.when(z >= s)
        def _():
            place_block(s, z - s)

        @pl.when(z + s < ZL)
        def _():
            place_block(s + ZL - 1, z + s)

    def part(p, carry):
        for copy in token_copies(p):
            copy.wait()
        both = jnp.dot(tokens[p], weights[...], preferred_element_type=jnp.float32)
        gate, up = both[:, :256], both[:, 256:]
        value = (gate / (1.0 + jnp.exp(-gate)) * up).astype(jnp.bfloat16)
        proj = lax.dot_general(
            factor_ref[...], value, (((1,), (1,)), ((), ())),
            preferred_element_type=jnp.float32,
        )
        space = jnp.zeros((proj.shape[0], 256 - half), jnp.float32)
        proj = jnp.concatenate([proj[:, :half], space, proj[:, half:], space], axis=1)
        lanes = pl.ds(pl.multiple_of(p * 512, 512), 512)
        for d in range(out_ref.shape[0]):
            out_ref[d, :, lanes] = proj[2 * d : 2 * d + 2]
        return carry

    lax.fori_loop(0, Y, part, 0)


def layer(place, factor, blocks, tokens):
    _, half, depth = tokens.shape
    cols = blocks[0].shape[1]
    rank = factor.shape[0]
    vmem = pl.BlockSpec(memory_space=pltpu.VMEM)
    return pl.pallas_call(
        layer_kernel,
        out_shape=jax.ShapeDtypeStruct((rank // 2, 2, Y * 512), jnp.float32),
        in_specs=[pl.BlockSpec(memory_space=pltpu.SMEM)]
        + [vmem] * (1 + len(blocks))
        + [pl.BlockSpec(memory_space=pl.ANY)],
        out_specs=vmem,
        scratch_shapes=[
            pltpu.VMEM((depth, 512), jnp.bfloat16),
            pltpu.VMEM((Y, 2 * half, depth), jnp.bfloat16),
            pltpu.SemaphoreType.DMA((Y, 2)),
        ],
        compiler_params=pltpu.CompilerParams(vmem_limit_bytes=38 * 2**20),
        cost_estimate=pl.CostEstimate(
            flops=4 * Y * half * cols * depth,
            bytes_accessed=2 * depth * (cols + 2 * Y * half),
            transcendentals=0,
        ),
        name="layer",
    )(place, factor, *blocks, tokens)


def tie(value, *after):
    return lax.optimization_barrier((value,) + after)[0]


class Chain:
    def __init__(self, block):
        self.ups, self.downs = [block], [block]

    def step(self):
        s = len(self.ups)
        up, down = self.ups[-1], self.downs[-1]
        if s > 2:
            up, down = tie(up, self.downs[-2]), tie(down, self.ups[-2])
        self.ups.append(lax.ppermute(up, "zl", [(z, z + 1) for z in range(s - 1, ZL - 1)]))
        self.downs.append(lax.ppermute(down, "zl", [(z, z - 1) for z in range(1, ZL + 1 - s)]))

    def after(self, *values):
        self.ups[-1] = tie(self.ups[-1], *values)
        self.downs[-1] = tie(self.downs[-1], *values)

    def join(self, value):
        self.ups[-1], self.downs[-1], value = lax.optimization_barrier(
            (self.ups[-1], self.downs[-1], value)
        )
        return value

    def blocks(self):
        return self.ups + self.downs[1:]


def weight_quarters(gate_weight, up_weight):
    depth, cols = gate_weight.shape
    return jnp.concatenate(
        [w.T.reshape(Y, cols // Y, depth) for w in (gate_weight, up_weight)], axis=1
    )


def out_partial(out_grad, out_factor):
    half = out_grad.shape[0] // 2
    grads = jnp.pad(out_grad.reshape(2, half, -1), ((0, 0), (0, 256 - half), (0, 0)))
    return lax.dot_general(
        out_factor, grads.reshape(512, -1), (((0,), (1,)), ((), ())),
        preferred_element_type=jnp.float32,
    )


def exchange_z(out, queries):
    rows, cols = queries.shape
    high = lax.reduce_precision(out, 8, 7)
    sent = jnp.concatenate(
        [v.astype(jnp.bfloat16) for v in (high, out - high)] + [queries.reshape(-1, out.shape[1])]
    )
    got = lax.all_gather(sent, "zh")
    count = out.shape[0]
    parts = got[:, : 2 * count].astype(jnp.float32)
    out = (parts[:, :count] + parts[:, count:]).sum(0)
    return out, got[:, 2 * count :].reshape(ZH, rows, cols)


def share_plane(out, queries):
    high = lax.reduce_precision(out, 8, 7)
    sent = jnp.concatenate(
        [v.astype(jnp.bfloat16) for v in (high, out - high)]
        + [queries.reshape(-1, out.shape[1])]
    )
    return lax.all_gather(sent, PLANE)


def unpack_queries(got, first, rows, cols):
    here = got.reshape((Y, X * C) + got.shape[1:])
    here = lax.dynamic_index_in_dim(here, lax.axis_index("y"), 0, keepdims=False)
    queries = here[:, first:].reshape(X, C, ZH, rows, cols)
    return queries.transpose(3, 0, 2, 1, 4).reshape(rows, -1)


def shards(tokens, gate_weight, up_weight, out_grad, in_factor, out_factor, queries):
    rows = tokens.shape[0]
    rank = in_factor.shape[1]
    half = rows // 2
    z, y, c = (lax.axis_index(name) for name in ("zl", "y", "c"))
    mine = lax.dynamic_slice_in_dim(tokens, c * half, half, 0)
    plane_tokens = lax.all_gather(mine, ("y", "c"))
    quarter = in_factor.shape[0] // Y
    factor = lax.dynamic_slice_in_dim(in_factor, y * quarter, quarter, 0).T
    factor = jnp.pad(factor, ((0, 0), (0, 256 - quarter)))

    quarters = weight_quarters(gate_weight, up_weight)
    chain = Chain(lax.all_to_all(quarters, "y", 0, 0, tiled=True))
    out = out_partial(out_grad, out_factor).reshape(X * C, rank // (X * C), -1)
    for s in range(1, ZL):
        chain.step()
        if s == 2:
            out = lax.all_to_all(out, ("x", "c"), 0, 0, tiled=True).sum(0)
        if s < 3:
            out = chain.join(out)
        if s == 6:
            out = chain.join(out)
        if s == 7:
            out, query_rows = chain.join(exchange_z(out, queries))
    shared = share_plane(out, query_rows)
    out = share(out, PLANE, Y * X * C)

    place = jnp.stack([z]).astype(jnp.int32)
    in_part = layer(place, factor, chain.blocks(), plane_tokens)
    in_part, out = lax.optimization_barrier((in_part, out))
    out = out.reshape(Y, rank, -1).transpose(1, 0, 2).reshape(rank, -1)
    in_proj = lax.all_to_all(in_part, PLANE, 0, 0, tiled=True)
    in_proj = in_proj.sum(0)

    seqs = Y * rows // LEN
    lane = jnp.arange(in_proj.shape[1])
    token = lane // 256 * half + lane % 256
    mask = (token // LEN)[None, :] == jnp.arange(seqs)[:, None]
    spread = jnp.where(mask[:, None, :], in_proj[None], 0.0).reshape(2 * seqs, -1)
    fragment = jnp.dot(spread, out.T, precision=HIGHEST) / jnp.sqrt(jnp.float32(LEN))
    fragment = fragment.reshape(seqs, 2 * rank)
    columns = share(fragment, ("zh", "zl"), ZH * ZL)
    columns, shared = lax.optimization_barrier((columns, shared))
    columns = columns.reshape(ZH, ZL * seqs, 2 * rank).sum(0).astype(jnp.bfloat16)
    query_rows = unpack_queries(shared, 2 * rank // (X * C), *queries.shape)
    features = share(columns, PLANE, Y * X * C)
    return solve(features, query_rows)


def solution(mesh):
    fine = Mesh(mesh.devices.reshape(ZL, Y, X, ZH, C), ("zl", "y", "x", "zh", "c"))
    dp, tensor = ("zl", "y"), ("x", "zh", "c")
    in_specs = (
        P(dp, None),
        P(dp, tensor),
        P(dp, tensor),
        P(dp, tensor),
        P(tensor, None),
        P(tensor, None),
        P(dp, tensor),
    )
    return jax.shard_map(
        shards, mesh=fine, in_specs=in_specs, out_specs=P(dp, None), check_vma=False
    )
```

```python
import functools

import jax
import jax.numpy as jnp
from jax import lax
from jax.experimental import pallas as pl
from jax.experimental.pallas import tpu as pltpu
from jax.sharding import Mesh, PartitionSpec as P

LEN = 160
DAMPING = 0.1
ZL, Y, X, ZH, C = 8, 4, 4, 2, 2
PLANE = ("y", "x", "c")
HIGHEST = lax.Precision.HIGHEST


def solve_body(features_ref, queries_ref, out_ref):
    blocks, count, width = features_ref.shape
    total = blocks * width
    features = jnp.concatenate([features_ref[d] for d in range(blocks)], axis=1)
    both = jnp.concatenate([features, queries_ref[...]], axis=0)
    system = lax.dot_general(
        features, both, (((1,), (1,)), ((), ())), preferred_element_type=jnp.float32
    )
    row = lax.broadcasted_iota(jnp.int32, system.shape, 0)
    lane = lax.broadcasted_iota(jnp.int32, system.shape, 1)
    system = jnp.where(
        lane < count,
        system / total + jnp.where(row == lane, DAMPING, 0.0),
        system / (total**0.5),
    )
    on_diagonal = jnp.where(row == lane, system, 0.0)
    row_scale = lax.rsqrt(jnp.sum(on_diagonal, axis=1, keepdims=True))
    lane_scale = jnp.sum(jnp.where(row == lane, row_scale, 0.0), axis=0, keepdims=True)
    system = system * row_scale * jnp.where(lane < count, lane_scale, 1.0)
    groups = [system[8 * g : 8 * g + 8] for g in range(count // 8)]
    inner = lax.broadcasted_iota(jnp.int32, groups[0].shape, 0)
    whole = groups[0].shape
    side = 4
    for low in range(0, len(groups), side):
        inside = groups[low : low + side]
        for k in range(8 * low, 8 * (low + side), 2):
            g, r = k // 8 - low, k % 8
            p = jnp.broadcast_to(inside[g][r : r + 1], whole)
            q = jnp.broadcast_to(inside[g][r + 1 : r + 2], whole)
            a, b, c, d = (
                jnp.broadcast_to(v[:, n : n + 1], whole) for v in (p, q) for n in (k, k + 1)
            )
            inverse = 1.0 / (a * d - b * c)
            first = (d * inverse) * p - (b * inverse) * q
            second = (a * inverse) * q - (c * inverse) * p
            updated = [
                block
                - jnp.broadcast_to(block[:, k : k + 1], whole) * first
                - jnp.broadcast_to(block[:, k + 1 : k + 2], whole) * second
                for block in inside
            ]
            updated[g] = jnp.where(
                inner == r, first, jnp.where(inner == r + 1, second, updated[g])
            )
            inside = updated
        rest = jnp.concatenate(groups[:low] + groups[low + side :], axis=0)
        rest = rest - lax.dot_general(
            rest[:, 8 * low : 8 * (low + side)], jnp.concatenate(inside, axis=0),
            (((1,), (0,)), ((), ())),
            precision=HIGHEST, preferred_element_type=jnp.float32,
        )
        rest = [rest[8 * n : 8 * n + 8] for n in range(len(groups) - side)]
        groups = rest[:low] + inside + rest[low:]
    groups = [block * row_scale[8 * g : 8 * g + 8] for g, block in enumerate(groups)]
    width = system.shape[1]
    groups += [jnp.zeros_like(groups[0])] * (width // 8 - len(groups))
    solved = jnp.concatenate(groups, axis=0).T
    out_ref[...] = solved[count:, :count]


def solve(features, queries):
    count = features.shape[1]
    return pl.pallas_call(
        solve_body,
        out_shape=jax.ShapeDtypeStruct((queries.shape[0], count), jnp.float32),
        compiler_params=pltpu.CompilerParams(vmem_limit_bytes=32 * 2**20),
        name="solve",
    )(features, queries)


def share(x, axes, count):
    return lax.all_to_all(
        jnp.broadcast_to(x[None], (count,) + x.shape), axes, 0, 0, tiled=True
    )


def layer_kernel(place_ref, factor_ref, *refs):
    chains = 2 * ZL - 1
    blocks = refs[:chains]
    all_tokens, out_ref, weights, tokens, token_sems = refs[chains:]
    z = place_ref[0]
    hidden = blocks[0].shape[1] // 2
    half = all_tokens.shape[1]

    def token_copies(p):
        for c in range(2):
            yield pltpu.make_async_copy(
                all_tokens.at[2 * p + c], tokens.at[p, pl.ds(c * half, half)], token_sems.at[p, c]
            )

    for p in range(Y):
        for copy in token_copies(p):
            copy.start()

    gap = jnp.zeros((256 - hidden, 128), jnp.bfloat16)

    def place_block(at, owner):
        for k in range(Y):
            block = blocks[at][k]
            wide = jnp.concatenate([block[:hidden], gap, block[hidden:], gap], axis=0)
            weights[pl.ds(pl.multiple_of((owner * Y + k) * 128, 128), 128), :] = wide.T

    place_block(0, z)
    for s in range(1, ZL):
        @pl.when(z >= s)
        def _():
            place_block(s, z - s)

        @pl.when(z + s < ZL)
        def _():
            place_block(s + ZL - 1, z + s)

    def part(p, carry):
        for copy in token_copies(p):
            copy.wait()
        both = jnp.dot(tokens[p], weights[...], preferred_element_type=jnp.float32)
        gate, up = both[:, :256], both[:, 256:]
        value = (gate / (1.0 + jnp.exp(-gate)) * up).astype(jnp.bfloat16)
        proj = lax.dot_general(
            factor_ref[...], value, (((1,), (1,)), ((), ())),
            preferred_element_type=jnp.float32,
        )
        space = jnp.zeros((proj.shape[0], 256 - half), jnp.float32)
        proj = jnp.concatenate([proj[:, :half], space, proj[:, half:], space], axis=1)
        lanes = pl.ds(pl.multiple_of(p * 512, 512), 512)
        for d in range(out_ref.shape[0]):
            out_ref[d, :, lanes] = proj[2 * d : 2 * d + 2]
        return carry

    lax.fori_loop(0, Y, part, 0)


def layer(place, factor, blocks, tokens):
    _, half, depth = tokens.shape
    cols = blocks[0].shape[1]
    rank = factor.shape[0]
    vmem = pl.BlockSpec(memory_space=pltpu.VMEM)
    return pl.pallas_call(
        layer_kernel,
        out_shape=jax.ShapeDtypeStruct((rank // 2, 2, Y * 512), jnp.float32),
        in_specs=[pl.BlockSpec(memory_space=pltpu.SMEM)]
        + [vmem] * (1 + len(blocks))
        + [pl.BlockSpec(memory_space=pl.ANY)],
        out_specs=vmem,
        scratch_shapes=[
            pltpu.VMEM((depth, 512), jnp.bfloat16),
            pltpu.VMEM((Y, 2 * half, depth), jnp.bfloat16),
            pltpu.SemaphoreType.DMA((Y, 2)),
        ],
        compiler_params=pltpu.CompilerParams(vmem_limit_bytes=38 * 2**20),
        cost_estimate=pl.CostEstimate(
            flops=4 * Y * half * cols * depth,
            bytes_accessed=2 * depth * (cols + 2 * Y * half),
            transcendentals=0,
        ),
        name="layer",
    )(place, factor, *blocks, tokens)


def tie(value, *after):
    return lax.optimization_barrier((value,) + after)[0]


class Chain:
    def __init__(self, block):
        self.ups, self.downs = [block], [block]

    def step(self):
        s = len(self.ups)
        up, down = self.ups[-1], self.downs[-1]
        if s > 2:
            up, down = tie(up, self.downs[-2]), tie(down, self.ups[-2])
        self.ups.append(lax.ppermute(up, "zl", [(z, z + 1) for z in range(s - 1, ZL - 1)]))
        self.downs.append(lax.ppermute(down, "zl", [(z, z - 1) for z in range(1, ZL + 1 - s)]))

    def after(self, *values):
        self.ups[-1] = tie(self.ups[-1], *values)
        self.downs[-1] = tie(self.downs[-1], *values)

    def blocks(self):
        return self.ups + self.downs[1:]


def weight_quarters(gate_weight, up_weight):
    depth, cols = gate_weight.shape
    return jnp.concatenate(
        [w.T.reshape(Y, cols // Y, depth) for w in (gate_weight, up_weight)], axis=1
    )


def out_partial(out_grad, out_factor):
    half = out_grad.shape[0] // 2
    grads = jnp.pad(out_grad.reshape(2, half, -1), ((0, 0), (0, 256 - half), (0, 0)))
    return lax.dot_general(
        out_factor, grads.reshape(512, -1), (((0,), (1,)), ((), ())),
        preferred_element_type=jnp.float32,
    )


def exchange_z(out, queries):
    rows, cols = queries.shape
    high = lax.reduce_precision(out, 8, 7)
    sent = jnp.concatenate(
        [v.astype(jnp.bfloat16) for v in (high, out - high)] + [queries.reshape(-1, out.shape[1])]
    )
    got = lax.all_gather(sent, "zh")
    count = out.shape[0]
    parts = got[:, : 2 * count].astype(jnp.float32)
    out = (parts[:, :count] + parts[:, count:]).sum(0)
    return out, got[:, 2 * count :].reshape(ZH, rows, cols)


def share_plane(out, queries):
    high = lax.reduce_precision(out, 8, 7)
    sent = jnp.concatenate(
        [v.astype(jnp.bfloat16) for v in (high, out - high)]
        + [queries.reshape(-1, out.shape[1])]
    )
    return lax.all_gather(sent, PLANE)


def unpack_queries(got, first, rows, cols):
    here = got.reshape((Y, X * C) + got.shape[1:])
    here = lax.dynamic_index_in_dim(here, lax.axis_index("y"), 0, keepdims=False)
    queries = here[:, first:].reshape(X, C, ZH, rows, cols)
    return queries.transpose(3, 0, 2, 1, 4).reshape(rows, -1)


def shards(tokens, gate_weight, up_weight, out_grad, in_factor, out_factor, queries):
    rows = tokens.shape[0]
    rank = in_factor.shape[1]
    half = rows // 2
    z, y, c = (lax.axis_index(name) for name in ("zl", "y", "c"))
    mine = lax.dynamic_slice_in_dim(tokens, c * half, half, 0)
    plane_tokens = lax.all_gather(mine, ("y", "c"))
    quarter = in_factor.shape[0] // Y
    factor = lax.dynamic_slice_in_dim(in_factor, y * quarter, quarter, 0).T
    factor = jnp.pad(factor, ((0, 0), (0, 256 - quarter)))

    quarters = weight_quarters(gate_weight, up_weight)
    chain = Chain(lax.all_to_all(quarters, "y", 0, 0, tiled=True))
    out = out_partial(out_grad, out_factor).reshape(X * C, rank // (X * C), -1)
    for s in range(1, ZL):
        chain.step()
        if s == 1:
            out = tie(out, chain.ups[-1])
            out = lax.all_to_all(out, ("x", "c"), 0, 0, tiled=True).sum(0)
        if s == 5:
            chain.after(out)
            out = tie(out, chain.ups[-1])
            out, query_rows = exchange_z(out, queries)
        if s == 6:
            shared = share_plane(out, query_rows)
            chain.after(out, plane_tokens)
            out = tie(out, chain.ups[-1])
            out = share(out, PLANE, Y * X * C)
    out = out.reshape(Y, rank, -1).transpose(1, 0, 2).reshape(rank, -1)

    place = jnp.stack([z]).astype(jnp.int32)
    in_part = layer(place, factor, chain.blocks(), plane_tokens)
    in_proj = lax.all_to_all(in_part, PLANE, 0, 0, tiled=True)
    in_proj = in_proj.sum(0)

    seqs = Y * rows // LEN
    lane = jnp.arange(in_proj.shape[1])
    token = lane // 256 * half + lane % 256
    mask = (token // LEN)[None, :] == jnp.arange(seqs)[:, None]
    spread = jnp.where(mask[:, None, :], in_proj[None], 0.0).reshape(2 * seqs, -1)
    fragment = jnp.dot(spread, out.T, precision=HIGHEST) / jnp.sqrt(jnp.float32(LEN))
    fragment = fragment.reshape(seqs, 2 * rank)
    columns = share(fragment, ("zh", "zl"), ZH * ZL)
    columns, shared = lax.optimization_barrier((columns, shared))
    columns = columns.reshape(ZH, ZL * seqs, 2 * rank).sum(0).astype(jnp.bfloat16)
    query_rows = unpack_queries(shared, 2 * rank // (X * C), *queries.shape)
    features = share(columns, PLANE, Y * X * C)
    return solve(features, query_rows)


def solution(mesh):
    fine = Mesh(mesh.devices.reshape(ZL, Y, X, ZH, C), ("zl", "y", "x", "zh", "c"))
    dp, tensor = ("zl", "y"), ("x", "zh", "c")
    in_specs = (
        P(dp, None),
        P(dp, tensor),
        P(dp, tensor),
        P(dp, tensor),
        P(tensor, None),
        P(tensor, None),
        P(dp, tensor),
    )
    return jax.shard_map(
        shards, mesh=fine, in_specs=in_specs, out_specs=P(dp, None), check_vma=False
    )
```

```python
import functools

import jax
import jax.numpy as jnp
from jax import lax
from jax.experimental import pallas as pl
from jax.experimental.pallas import tpu as pltpu
from jax.sharding import Mesh, PartitionSpec as P

LEN = 160
DAMPING = 0.1
ZL, Y, X, ZH, C = 8, 4, 4, 2, 2
PLANE = ("y", "x", "c")
HIGHEST = lax.Precision.HIGHEST


def solve_body(features_ref, queries_ref, out_ref):
    blocks, count, width = features_ref.shape
    total = blocks * width
    features = jnp.concatenate([features_ref[d] for d in range(blocks)], axis=1)
    both = jnp.concatenate([features, queries_ref[...]], axis=0)
    system = lax.dot_general(
        features, both, (((1,), (1,)), ((), ())), preferred_element_type=jnp.float32
    )
    row = lax.broadcasted_iota(jnp.int32, system.shape, 0)
    lane = lax.broadcasted_iota(jnp.int32, system.shape, 1)
    system = jnp.where(
        lane < count,
        system / total + jnp.where(row == lane, DAMPING, 0.0),
        system / (total**0.5),
    )
    on_diagonal = jnp.where(row == lane, system, 0.0)
    row_scale = lax.rsqrt(jnp.sum(on_diagonal, axis=1, keepdims=True))
    lane_scale = jnp.sum(jnp.where(row == lane, row_scale, 0.0), axis=0, keepdims=True)
    system = system * row_scale * jnp.where(lane < count, lane_scale, 1.0)
    groups = [system[8 * g : 8 * g + 8] for g in range(count // 8)]
    inner = lax.broadcasted_iota(jnp.int32, groups[0].shape, 0)
    whole = groups[0].shape
    side = 4
    for low in range(0, len(groups), side):
        inside = groups[low : low + side]
        for k in range(8 * low, 8 * (low + side), 2):
            g, r = k // 8 - low, k % 8
            p = jnp.broadcast_to(inside[g][r : r + 1], whole)
            q = jnp.broadcast_to(inside[g][r + 1 : r + 2], whole)
            a, b, c, d = (
                jnp.broadcast_to(v[:, n : n + 1], whole) for v in (p, q) for n in (k, k + 1)
            )
            inverse = 1.0 / (a * d - b * c)
            first = (d * inverse) * p - (b * inverse) * q
            second = (a * inverse) * q - (c * inverse) * p
            updated = [
                block
                - jnp.broadcast_to(block[:, k : k + 1], whole) * first
                - jnp.broadcast_to(block[:, k + 1 : k + 2], whole) * second
                for block in inside
            ]
            updated[g] = jnp.where(
                inner == r, first, jnp.where(inner == r + 1, second, updated[g])
            )
            inside = updated
        rest = jnp.concatenate(groups[:low] + groups[low + side :], axis=0)
        rest = rest - lax.dot_general(
            rest[:, 8 * low : 8 * (low + side)], jnp.concatenate(inside, axis=0),
            (((1,), (0,)), ((), ())),
            precision=HIGHEST, preferred_element_type=jnp.float32,
        )
        rest = [rest[8 * n : 8 * n + 8] for n in range(len(groups) - side)]
        groups = rest[:low] + inside + rest[low:]
    groups = [block * row_scale[8 * g : 8 * g + 8] for g, block in enumerate(groups)]
    width = system.shape[1]
    groups += [jnp.zeros_like(groups[0])] * (width // 8 - len(groups))
    solved = jnp.concatenate(groups, axis=0).T
    out_ref[...] = solved[count:, :count]


def solve(features, queries):
    count = features.shape[1]
    return pl.pallas_call(
        solve_body,
        out_shape=jax.ShapeDtypeStruct((queries.shape[0], count), jnp.float32),
        compiler_params=pltpu.CompilerParams(vmem_limit_bytes=32 * 2**20),
        name="solve",
    )(features, queries)


def share(x, axes, count):
    return lax.all_to_all(
        jnp.broadcast_to(x[None], (count,) + x.shape), axes, 0, 0, tiled=True
    )


def layer_kernel(place_ref, factor_ref, *refs):
    chains = 2 * ZL - 1
    blocks = refs[:chains]
    all_tokens, out_ref, weights, tokens, token_sems = refs[chains:]
    z = place_ref[0]
    hidden = blocks[0].shape[1] // 2
    half = all_tokens.shape[1]

    parts, pieces = token_sems.shape

    def token_copies(p):
        for c in range(pieces):
            yield pltpu.make_async_copy(
                all_tokens.at[pieces * p + c],
                tokens.at[p, pl.ds(c * half, half)],
                token_sems.at[p, c],
            )

    for p in range(parts):
        for copy in token_copies(p):
            copy.start()

    gap = jnp.zeros((256 - hidden, 128), jnp.bfloat16)

    def place_block(at, owner):
        for k in range(Y):
            block = blocks[at][k]
            wide = jnp.concatenate([block[:hidden], gap, block[hidden:], gap], axis=0)
            weights[pl.ds(pl.multiple_of((owner * Y + k) * 128, 128), 128), :] = wide.T

    place_block(0, z)
    for s in range(1, ZL):
        @pl.when(z >= s)
        def _():
            place_block(s, z - s)

        @pl.when(z + s < ZL)
        def _():
            place_block(s + ZL - 1, z + s)

    def part(p, carry):
        for copy in token_copies(p):
            copy.wait()
        both = jnp.dot(tokens[p], weights[...], preferred_element_type=jnp.float32)
        gate, up = both[:, :256], both[:, 256:]
        value = (gate / (1.0 + jnp.exp(-gate)) * up).astype(jnp.bfloat16)
        proj = lax.dot_general(
            factor_ref[...], value, (((1,), (1,)), ((), ())),
            preferred_element_type=jnp.float32,
        )
        space = jnp.zeros((proj.shape[0], 256 - half), jnp.float32)
        spread = []
        for c in range(pieces):
            spread += [proj[:, c * half : (c + 1) * half], space]
        proj = jnp.concatenate(spread, axis=1)
        lanes = pl.ds(pl.multiple_of(p * (256 * pieces), 256), 256 * pieces)
        for d in range(out_ref.shape[0]):
            out_ref[d, :, lanes] = proj[2 * d : 2 * d + 2]
        return carry

    lax.fori_loop(0, parts, part, 0)


def layer(place, factor, blocks, tokens):
    _, half, depth = tokens.shape
    cols = blocks[0].shape[1]
    rank = factor.shape[0]
    vmem = pl.BlockSpec(memory_space=pltpu.VMEM)
    return pl.pallas_call(
        layer_kernel,
        out_shape=jax.ShapeDtypeStruct((rank // 2, 2, Y * 512), jnp.float32),
        in_specs=[pl.BlockSpec(memory_space=pltpu.SMEM)]
        + [vmem] * (1 + len(blocks))
        + [pl.BlockSpec(memory_space=pl.ANY)],
        out_specs=vmem,
        scratch_shapes=[
            pltpu.VMEM((depth, 512), jnp.bfloat16),
            pltpu.VMEM((Y // 2, 4 * half, depth), jnp.bfloat16),
            pltpu.SemaphoreType.DMA((Y // 2, 4)),
        ],
        compiler_params=pltpu.CompilerParams(vmem_limit_bytes=38 * 2**20),
        cost_estimate=pl.CostEstimate(
            flops=4 * Y * half * cols * depth,
            bytes_accessed=2 * depth * (cols + 2 * Y * half),
            transcendentals=0,
        ),
        name="layer",
    )(place, factor, *blocks, tokens)


def tie(value, *after):
    return lax.optimization_barrier((value,) + after)[0]


class Chain:
    def __init__(self, block):
        self.ups, self.downs = [block], [block]

    def step(self):
        s = len(self.ups)
        up, down = self.ups[-1], self.downs[-1]
        if s > 2:
            up, down = tie(up, self.downs[-2]), tie(down, self.ups[-2])
        self.ups.append(lax.ppermute(up, "zl", [(z, z + 1) for z in range(s - 1, ZL - 1)]))
        self.downs.append(lax.ppermute(down, "zl", [(z, z - 1) for z in range(1, ZL + 1 - s)]))

    def after(self, *values):
        self.ups[-1] = tie(self.ups[-1], *values)
        self.downs[-1] = tie(self.downs[-1], *values)

    def blocks(self):
        return self.ups + self.downs[1:]


def weight_quarters(gate_weight, up_weight):
    depth, cols = gate_weight.shape
    return jnp.concatenate(
        [w.T.reshape(Y, cols // Y, depth) for w in (gate_weight, up_weight)], axis=1
    )


def out_partial(out_grad, out_factor):
    half = out_grad.shape[0] // 2
    grads = jnp.pad(out_grad.reshape(2, half, -1), ((0, 0), (0, 256 - half), (0, 0)))
    return lax.dot_general(
        out_factor, grads.reshape(512, -1), (((0,), (1,)), ((), ())),
        preferred_element_type=jnp.float32,
    )


def exchange_z(out, queries):
    rows, cols = queries.shape
    high = lax.reduce_precision(out, 8, 7)
    sent = jnp.concatenate(
        [v.astype(jnp.bfloat16) for v in (high, out - high)] + [queries.reshape(-1, out.shape[1])]
    )
    got = lax.all_gather(sent, "zh")
    count = out.shape[0]
    parts = got[:, : 2 * count].astype(jnp.float32)
    out = (parts[:, :count] + parts[:, count:]).sum(0)
    return out, got[:, 2 * count :].reshape(ZH, rows, cols)


def share_plane(out, queries):
    high = lax.reduce_precision(out, 8, 7)
    sent = jnp.concatenate(
        [v.astype(jnp.bfloat16) for v in (high, out - high)]
        + [queries.reshape(-1, out.shape[1])]
    )
    return lax.all_gather(sent, PLANE)


def unpack_queries(got, first, rows, cols):
    here = got.reshape((Y, X * C) + got.shape[1:])
    here = lax.dynamic_index_in_dim(here, lax.axis_index("y"), 0, keepdims=False)
    queries = here[:, first:].reshape(X, C, ZH, rows, cols)
    return queries.transpose(3, 0, 2, 1, 4).reshape(rows, -1)


def shards(tokens, gate_weight, up_weight, out_grad, in_factor, out_factor, queries):
    rows = tokens.shape[0]
    rank = in_factor.shape[1]
    half = rows // 2
    z, y, c = (lax.axis_index(name) for name in ("zl", "y", "c"))
    mine = lax.dynamic_slice_in_dim(tokens, c * half, half, 0)
    plane_tokens = lax.all_gather(mine, ("y", "c"))
    quarter = in_factor.shape[0] // Y
    factor = lax.dynamic_slice_in_dim(in_factor, y * quarter, quarter, 0).T
    factor = jnp.pad(factor, ((0, 0), (0, 256 - quarter)))

    quarters = weight_quarters(gate_weight, up_weight)
    chain = Chain(lax.all_to_all(quarters, "y", 0, 0, tiled=True))
    out = out_partial(out_grad, out_factor).reshape(X * C, rank // (X * C), -1)
    for s in range(1, ZL):
        chain.step()
        if s == 1:
            out = tie(out, chain.ups[-1])
            out = lax.all_to_all(out, ("x", "c"), 0, 0, tiled=True).sum(0)
        if s == 5:
            chain.after(out)
            out = tie(out, chain.ups[-1])
            out, query_rows = exchange_z(out, queries)
        if s == 6:
            shared = share_plane(out, query_rows)
            chain.after(out, plane_tokens)
            out = tie(out, chain.ups[-1])
            out = share(out, PLANE, Y * X * C)
    out = out.reshape(Y, rank, -1).transpose(1, 0, 2).reshape(rank, -1)

    place = jnp.stack([z]).astype(jnp.int32)
    in_part = layer(place, factor, chain.blocks(), plane_tokens)
    in_proj = lax.all_to_all(in_part, PLANE, 0, 0, tiled=True)
    in_proj = in_proj.sum(0)

    seqs = Y * rows // LEN
    lane = jnp.arange(in_proj.shape[1])
    token = lane // 256 * half + lane % 256
    mask = (token // LEN)[None, :] == jnp.arange(seqs)[:, None]
    spread = jnp.where(mask[:, None, :], in_proj[None], 0.0).reshape(2 * seqs, -1)
    fragment = jnp.dot(spread, out.T, precision=HIGHEST) / jnp.sqrt(jnp.float32(LEN))
    fragment = fragment.reshape(seqs, 2 * rank)
    columns = share(fragment, ("zh", "zl"), ZH * ZL)
    columns, shared = lax.optimization_barrier((columns, shared))
    columns = columns.reshape(ZH, ZL * seqs, 2 * rank).sum(0).astype(jnp.bfloat16)
    query_rows = unpack_queries(shared, 2 * rank // (X * C), *queries.shape)
    features = share(columns, PLANE, Y * X * C)
    return solve(features, query_rows)


def solution(mesh):
    fine = Mesh(mesh.devices.reshape(ZL, Y, X, ZH, C), ("zl", "y", "x", "zh", "c"))
    dp, tensor = ("zl", "y"), ("x", "zh", "c")
    in_specs = (
        P(dp, None),
        P(dp, tensor),
        P(dp, tensor),
        P(dp, tensor),
        P(tensor, None),
        P(tensor, None),
        P(dp, tensor),
    )
    return jax.shard_map(
        shards, mesh=fine, in_specs=in_specs, out_specs=P(dp, None), check_vma=False
    )
```

```python
import functools

import jax
import jax.numpy as jnp
from jax import lax
from jax.experimental import pallas as pl
from jax.experimental.pallas import tpu as pltpu
from jax.sharding import Mesh, PartitionSpec as P

LEN = 160
DAMPING = 0.1
ZL, Y, X, ZH, C = 8, 4, 4, 2, 2
PLANE = ("y", "x", "c")
HIGHEST = lax.Precision.HIGHEST


def solve_body(features_ref, queries_ref, out_ref):
    blocks, count, width = features_ref.shape
    total = blocks * width
    features = jnp.concatenate([features_ref[d] for d in range(blocks)], axis=1)
    both = jnp.concatenate([features, queries_ref[...]], axis=0)
    system = lax.dot_general(
        features, both, (((1,), (1,)), ((), ())), preferred_element_type=jnp.float32
    )
    row = lax.broadcasted_iota(jnp.int32, system.shape, 0)
    lane = lax.broadcasted_iota(jnp.int32, system.shape, 1)
    system = jnp.where(
        lane < count,
        system / total + jnp.where(row == lane, DAMPING, 0.0),
        system / (total**0.5),
    )
    on_diagonal = jnp.where(row == lane, system, 0.0)
    row_scale = lax.rsqrt(jnp.sum(on_diagonal, axis=1, keepdims=True))
    lane_scale = jnp.sum(jnp.where(row == lane, row_scale, 0.0), axis=0, keepdims=True)
    system = system * row_scale * jnp.where(lane < count, lane_scale, 1.0)
    groups = [system[8 * g : 8 * g + 8] for g in range(count // 8)]
    inner = lax.broadcasted_iota(jnp.int32, groups[0].shape, 0)
    whole = groups[0].shape
    side = 4
    for low in range(0, len(groups), side):
        inside = groups[low : low + side]
        for k in range(8 * low, 8 * (low + side), 2):
            g, r = k // 8 - low, k % 8
            p = jnp.broadcast_to(inside[g][r : r + 1], whole)
            q = jnp.broadcast_to(inside[g][r + 1 : r + 2], whole)
            a, b, c, d = (
                jnp.broadcast_to(v[:, n : n + 1], whole) for v in (p, q) for n in (k, k + 1)
            )
            inverse = 1.0 / (a * d - b * c)
            first = (d * inverse) * p - (b * inverse) * q
            second = (a * inverse) * q - (c * inverse) * p
            updated = [
                block
                - jnp.broadcast_to(block[:, k : k + 1], whole) * first
                - jnp.broadcast_to(block[:, k + 1 : k + 2], whole) * second
                for block in inside
            ]
            updated[g] = jnp.where(
                inner == r, first, jnp.where(inner == r + 1, second, updated[g])
            )
            inside = updated
        rest = jnp.concatenate(groups[:low] + groups[low + side :], axis=0)
        rest = rest - lax.dot_general(
            rest[:, 8 * low : 8 * (low + side)], jnp.concatenate(inside, axis=0),
            (((1,), (0,)), ((), ())),
            precision=HIGHEST, preferred_element_type=jnp.float32,
        )
        rest = [rest[8 * n : 8 * n + 8] for n in range(len(groups) - side)]
        groups = rest[:low] + inside + rest[low:]
    groups = [block * row_scale[8 * g : 8 * g + 8] for g, block in enumerate(groups)]
    width = system.shape[1]
    groups += [jnp.zeros_like(groups[0])] * (width // 8 - len(groups))
    solved = jnp.concatenate(groups, axis=0).T
    out_ref[...] = solved[count:, :count]


def solve(features, queries):
    count = features.shape[1]
    return pl.pallas_call(
        solve_body,
        out_shape=jax.ShapeDtypeStruct((queries.shape[0], count), jnp.float32),
        compiler_params=pltpu.CompilerParams(vmem_limit_bytes=32 * 2**20),
        name="solve",
    )(features, queries)


def share(x, axes, count):
    return lax.all_to_all(
        jnp.broadcast_to(x[None], (count,) + x.shape), axes, 0, 0, tiled=True
    )


def layer_kernel(place_ref, factor_ref, *refs):
    chains = 2 * ZL - 1
    blocks = refs[:chains]
    all_tokens, out_ref, weights, tokens, token_sems = refs[chains:]
    z = place_ref[0]
    hidden = blocks[0].shape[1] // 2
    half = all_tokens.shape[1]

    def token_copies(p):
        for c in range(2):
            yield pltpu.make_async_copy(
                all_tokens.at[2 * p + c], tokens.at[p, pl.ds(c * half, half)], token_sems.at[p, c]
            )

    for p in range(Y):
        for copy in token_copies(p):
            copy.start()

    gap = jnp.zeros((256 - hidden, 128), jnp.bfloat16)

    def place_block(at, owner):
        for k in range(Y):
            block = blocks[at][k]
            wide = jnp.concatenate([block[:hidden], gap, block[hidden:], gap], axis=0)
            weights[pl.ds(pl.multiple_of((owner * Y + k) * 128, 128), 128), :] = wide.T

    place_block(0, z)
    for s in range(1, ZL):
        @pl.when(z >= s)
        def _():
            place_block(s, z - s)

        @pl.when(z + s < ZL)
        def _():
            place_block(s + ZL - 1, z + s)

    def part(p, carry):
        for copy in token_copies(p):
            copy.wait()
        both = jnp.dot(tokens[p], weights[...], preferred_element_type=jnp.float32)
        gate, up = both[:, :256], both[:, 256:]
        value = (gate / (1.0 + jnp.exp(-gate)) * up).astype(jnp.bfloat16)
        proj = lax.dot_general(
            factor_ref[...], value, (((1,), (1,)), ((), ())),
            preferred_element_type=jnp.float32,
        )
        space = jnp.zeros((proj.shape[0], 256 - half), jnp.float32)
        proj = jnp.concatenate([proj[:, :half], space, proj[:, half:], space], axis=1)
        lanes = pl.ds(pl.multiple_of(p * 512, 512), 512)
        for d in range(out_ref.shape[0]):
            out_ref[d, :, lanes] = proj[2 * d : 2 * d + 2]
        return carry

    lax.fori_loop(0, Y, part, 0)


def layer(place, factor, blocks, tokens):
    _, half, depth = tokens.shape
    cols = blocks[0].shape[1]
    rank = factor.shape[0]
    vmem = pl.BlockSpec(memory_space=pltpu.VMEM)
    return pl.pallas_call(
        layer_kernel,
        out_shape=jax.ShapeDtypeStruct((rank // 2, 2, Y * 512), jnp.float32),
        in_specs=[pl.BlockSpec(memory_space=pltpu.SMEM)]
        + [vmem] * (1 + len(blocks))
        + [pl.BlockSpec(memory_space=pl.ANY)],
        out_specs=vmem,
        scratch_shapes=[
            pltpu.VMEM((depth, 512), jnp.bfloat16),
            pltpu.VMEM((Y, 2 * half, depth), jnp.bfloat16),
            pltpu.SemaphoreType.DMA((Y, 2)),
        ],
        compiler_params=pltpu.CompilerParams(vmem_limit_bytes=38 * 2**20),
        cost_estimate=pl.CostEstimate(
            flops=4 * Y * half * cols * depth,
            bytes_accessed=2 * depth * (cols + 2 * Y * half),
            transcendentals=0,
        ),
        name="layer",
    )(place, factor, *blocks, tokens)


def tie(value, *after):
    return lax.optimization_barrier((value,) + after)[0]


class Chain:
    def __init__(self, block):
        self.ups, self.downs = [block], [block]

    def step(self):
        s = len(self.ups)
        up, down = self.ups[-1], self.downs[-1]
        if s > 2:
            up, down = tie(up, self.downs[-2]), tie(down, self.ups[-2])
        self.ups.append(lax.ppermute(up, "zl", [(z, z + 1) for z in range(s - 1, ZL - 1)]))
        self.downs.append(lax.ppermute(down, "zl", [(z, z - 1) for z in range(1, ZL + 1 - s)]))

    def after(self, *values):
        self.ups[-1] = tie(self.ups[-1], *values)
        self.downs[-1] = tie(self.downs[-1], *values)

    def join(self, value):
        self.ups[-1], self.downs[-1], value = lax.optimization_barrier(
            (self.ups[-1], self.downs[-1], value)
        )
        return value

    def blocks(self):
        return self.ups + self.downs[1:]


def weight_quarters(gate_weight, up_weight):
    depth, cols = gate_weight.shape
    return jnp.concatenate(
        [w.T.reshape(Y, cols // Y, depth) for w in (gate_weight, up_weight)], axis=1
    )


def out_partial(out_grad, out_factor):
    half = out_grad.shape[0] // 2
    grads = jnp.pad(out_grad.reshape(2, half, -1), ((0, 0), (0, 256 - half), (0, 0)))
    return lax.dot_general(
        out_factor, grads.reshape(512, -1), (((0,), (1,)), ((), ())),
        preferred_element_type=jnp.float32,
    )


def exchange_z(out, queries):
    rows, cols = queries.shape
    high = lax.reduce_precision(out, 8, 7)
    sent = jnp.concatenate(
        [v.astype(jnp.bfloat16) for v in (high, out - high)] + [queries.reshape(-1, out.shape[1])]
    )
    got = lax.all_gather(sent, "zh")
    count = out.shape[0]
    parts = got[:, : 2 * count].astype(jnp.float32)
    out = (parts[:, :count] + parts[:, count:]).sum(0)
    return out, got[:, 2 * count :].reshape(ZH, rows, cols)


def share_plane(out, queries):
    high = lax.reduce_precision(out, 8, 7)
    sent = jnp.concatenate(
        [v.astype(jnp.bfloat16) for v in (high, out - high)]
        + [queries.reshape(-1, out.shape[1])]
    )
    return lax.all_gather(sent, PLANE)


def unpack_queries(got, first, rows, cols):
    here = got.reshape((Y, X * C) + got.shape[1:])
    here = lax.dynamic_index_in_dim(here, lax.axis_index("y"), 0, keepdims=False)
    queries = here[:, first:].reshape(X, C, ZH, rows, cols)
    return queries.transpose(3, 0, 2, 1, 4).reshape(rows, -1)


def shards(tokens, gate_weight, up_weight, out_grad, in_factor, out_factor, queries):
    rows = tokens.shape[0]
    rank = in_factor.shape[1]
    half = rows // 2
    z, y, c = (lax.axis_index(name) for name in ("zl", "y", "c"))
    mine = lax.dynamic_slice_in_dim(tokens, c * half, half, 0)
    plane_tokens = lax.all_gather(mine, ("y", "c"))
    quarter = in_factor.shape[0] // Y
    factor = lax.dynamic_slice_in_dim(in_factor, y * quarter, quarter, 0).T
    factor = jnp.pad(factor, ((0, 0), (0, 256 - quarter)))

    quarters = weight_quarters(gate_weight, up_weight)
    chain = Chain(lax.all_to_all(quarters, "y", 0, 0, tiled=True))
    out = out_partial(out_grad, out_factor).reshape(X * C, rank // (X * C), -1)
    for s in range(1, ZL):
        chain.step()
        if s == 1:
            out = tie(out, chain.ups[-1])
            out = lax.all_to_all(out, ("x", "c"), 0, 0, tiled=True).sum(0)
        if s == 5:
            chain.after(out)
        if s == 6:
            out = chain.join(out)
        if s == 7:
            out, query_rows = chain.join(exchange_z(out, queries))
    shared = share_plane(out, query_rows)
    out = share(out, PLANE, Y * X * C)

    place = jnp.stack([z]).astype(jnp.int32)
    in_part = layer(place, factor, chain.blocks(), plane_tokens)
    in_part, out = lax.optimization_barrier((in_part, out))
    out = out.reshape(Y, rank, -1).transpose(1, 0, 2).reshape(rank, -1)
    in_proj = lax.all_to_all(in_part, PLANE, 0, 0, tiled=True)
    in_proj = in_proj.sum(0)

    seqs = Y * rows // LEN
    lane = jnp.arange(in_proj.shape[1])
    token = lane // 256 * half + lane % 256
    mask = (token // LEN)[None, :] == jnp.arange(seqs)[:, None]
    spread = jnp.where(mask[:, None, :], in_proj[None], 0.0).reshape(2 * seqs, -1)
    fragment = jnp.dot(spread, out.T, precision=HIGHEST) / jnp.sqrt(jnp.float32(LEN))
    fragment = fragment.reshape(seqs, 2 * rank)
    columns = share(fragment, ("zh", "zl"), ZH * ZL)
    columns, shared = lax.optimization_barrier((columns, shared))
    columns = columns.reshape(ZH, ZL * seqs, 2 * rank).sum(0).astype(jnp.bfloat16)
    query_rows = unpack_queries(shared, 2 * rank // (X * C), *queries.shape)
    features = share(columns, PLANE, Y * X * C)
    return solve(features, query_rows)


def solution(mesh):
    fine = Mesh(mesh.devices.reshape(ZL, Y, X, ZH, C), ("zl", "y", "x", "zh", "c"))
    dp, tensor = ("zl", "y"), ("x", "zh", "c")
    in_specs = (
        P(dp, None),
        P(dp, tensor),
        P(dp, tensor),
        P(dp, tensor),
        P(tensor, None),
        P(tensor, None),
        P(dp, tensor),
    )
    return jax.shard_map(
        shards, mesh=fine, in_specs=in_specs, out_specs=P(dp, None), check_vma=False
    )
```

```python
import functools

import jax
import jax.numpy as jnp
from jax import lax
from jax.experimental import pallas as pl
from jax.experimental.pallas import tpu as pltpu
from jax.sharding import Mesh, PartitionSpec as P

LEN = 160
DAMPING = 0.1
ZL, Y, X, ZH, C = 8, 4, 4, 2, 2
PLANE = ("y", "x", "c")
HIGHEST = lax.Precision.HIGHEST


def solve_body(features_ref, queries_ref, out_ref):
    blocks, count, width = features_ref.shape
    total = blocks * width
    features = jnp.concatenate([features_ref[d] for d in range(blocks)], axis=1)
    both = jnp.concatenate([features, queries_ref[...]], axis=0)
    system = lax.dot_general(
        features, both, (((1,), (1,)), ((), ())), preferred_element_type=jnp.float32
    )
    row = lax.broadcasted_iota(jnp.int32, system.shape, 0)
    lane = lax.broadcasted_iota(jnp.int32, system.shape, 1)
    system = jnp.where(
        lane < count,
        system / total + jnp.where(row == lane, DAMPING, 0.0),
        system / (total**0.5),
    )
    on_diagonal = jnp.where(row == lane, system, 0.0)
    row_scale = lax.rsqrt(jnp.sum(on_diagonal, axis=1, keepdims=True))
    lane_scale = jnp.sum(jnp.where(row == lane, row_scale, 0.0), axis=0, keepdims=True)
    system = system * row_scale * jnp.where(lane < count, lane_scale, 1.0)
    groups = [system[8 * g : 8 * g + 8] for g in range(count // 8)]
    inner = lax.broadcasted_iota(jnp.int32, groups[0].shape, 0)
    whole = groups[0].shape
    side = 4
    for low in range(0, len(groups), side):
        inside = groups[low : low + side]
        for k in range(8 * low, 8 * (low + side), 2):
            g, r = k // 8 - low, k % 8
            p = jnp.broadcast_to(inside[g][r : r + 1], whole)
            q = jnp.broadcast_to(inside[g][r + 1 : r + 2], whole)
            a, b, c, d = (
                jnp.broadcast_to(v[:, n : n + 1], whole) for v in (p, q) for n in (k, k + 1)
            )
            inverse = 1.0 / (a * d - b * c)
            first = (d * inverse) * p - (b * inverse) * q
            second = (a * inverse) * q - (c * inverse) * p
            updated = [
                block
                - jnp.broadcast_to(block[:, k : k + 1], whole) * first
                - jnp.broadcast_to(block[:, k + 1 : k + 2], whole) * second
                for block in inside
            ]
            updated[g] = jnp.where(
                inner == r, first, jnp.where(inner == r + 1, second, updated[g])
            )
            inside = updated
        rest = jnp.concatenate(groups[:low] + groups[low + side :], axis=0)
        rest = rest - lax.dot_general(
            rest[:, 8 * low : 8 * (low + side)], jnp.concatenate(inside, axis=0),
            (((1,), (0,)), ((), ())),
            precision=HIGHEST, preferred_element_type=jnp.float32,
        )
        rest = [rest[8 * n : 8 * n + 8] for n in range(len(groups) - side)]
        groups = rest[:low] + inside + rest[low:]
    groups = [block * row_scale[8 * g : 8 * g + 8] for g, block in enumerate(groups)]
    width = system.shape[1]
    groups += [jnp.zeros_like(groups[0])] * (width // 8 - len(groups))
    solved = jnp.concatenate(groups, axis=0).T
    out_ref[...] = solved[count:, :count]


def solve(features, queries):
    count = features.shape[1]
    return pl.pallas_call(
        solve_body,
        out_shape=jax.ShapeDtypeStruct((queries.shape[0], count), jnp.float32),
        compiler_params=pltpu.CompilerParams(vmem_limit_bytes=32 * 2**20),
        name="solve",
    )(features, queries)


def share(x, axes, count):
    return lax.all_to_all(
        jnp.broadcast_to(x[None], (count,) + x.shape), axes, 0, 0, tiled=True
    )


def layer_kernel(place_ref, factor_ref, *refs):
    chains = 2 * ZL - 1
    blocks = refs[:chains]
    all_tokens, out_ref, weights, tokens, token_sems = refs[chains:]
    z = place_ref[0]
    hidden = blocks[0].shape[1] // 2
    half = all_tokens.shape[1]

    def token_copies(p):
        for c in range(2):
            yield pltpu.make_async_copy(
                all_tokens.at[2 * p + c], tokens.at[p, pl.ds(c * half, half)], token_sems.at[p, c]
            )

    for p in range(Y):
        for copy in token_copies(p):
            copy.start()

    gap = jnp.zeros((256 - hidden, 128), jnp.bfloat16)

    def place_block(at, owner):
        for k in range(Y):
            block = blocks[at][k]
            wide = jnp.concatenate([block[:hidden], gap, block[hidden:], gap], axis=0)
            weights[pl.ds(pl.multiple_of((owner * Y + k) * 128, 128), 128), :] = wide.T

    place_block(0, z)
    for s in range(1, ZL):
        @pl.when(z >= s)
        def _():
            place_block(s, z - s)

        @pl.when(z + s < ZL)
        def _():
            place_block(s + ZL - 1, z + s)

    def part(p, carry):
        for copy in token_copies(p):
            copy.wait()
        both = jnp.dot(tokens[p], weights[...], preferred_element_type=jnp.float32)
        gate, up = both[:, :256], both[:, 256:]
        value = (gate / (1.0 + jnp.exp(-gate)) * up).astype(jnp.bfloat16)
        proj = lax.dot_general(
            factor_ref[...], value, (((1,), (1,)), ((), ())),
            preferred_element_type=jnp.float32,
        )
        space = jnp.zeros((proj.shape[0], 256 - half), jnp.float32)
        proj = jnp.concatenate([proj[:, :half], space, proj[:, half:], space], axis=1)
        lanes = pl.ds(pl.multiple_of(p * 512, 512), 512)
        for d in range(out_ref.shape[0]):
            out_ref[d, :, lanes] = proj[2 * d : 2 * d + 2]
        return carry

    lax.fori_loop(0, Y, part, 0)


def layer(place, factor, blocks, tokens):
    _, half, depth = tokens.shape
    cols = blocks[0].shape[1]
    rank = factor.shape[0]
    vmem = pl.BlockSpec(memory_space=pltpu.VMEM)
    return pl.pallas_call(
        layer_kernel,
        out_shape=jax.ShapeDtypeStruct((rank // 2, 2, Y * 512), jnp.float32),
        in_specs=[pl.BlockSpec(memory_space=pltpu.SMEM)]
        + [vmem] * (1 + len(blocks))
        + [pl.BlockSpec(memory_space=pl.ANY)],
        out_specs=vmem,
        scratch_shapes=[
            pltpu.VMEM((depth, 512), jnp.bfloat16),
            pltpu.VMEM((Y, 2 * half, depth), jnp.bfloat16),
            pltpu.SemaphoreType.DMA((Y, 2)),
        ],
        compiler_params=pltpu.CompilerParams(vmem_limit_bytes=38 * 2**20),
        cost_estimate=pl.CostEstimate(
            flops=4 * Y * half * cols * depth,
            bytes_accessed=2 * depth * (cols + 2 * Y * half),
            transcendentals=0,
        ),
        name="layer",
    )(place, factor, *blocks, tokens)


def tie(value, *after):
    return lax.optimization_barrier((value,) + after)[0]


class Chain:
    def __init__(self, block):
        self.ups, self.downs = [block], [block]

    def step(self):
        s = len(self.ups)
        up, down = self.ups[-1], self.downs[-1]
        if s > 2:
            up, down = tie(up, self.downs[-2]), tie(down, self.ups[-2])
        self.ups.append(lax.ppermute(up, "zl", [(z, z + 1) for z in range(s - 1, ZL - 1)]))
        self.downs.append(lax.ppermute(down, "zl", [(z, z - 1) for z in range(1, ZL + 1 - s)]))

    def after(self, *values):
        self.ups[-1] = tie(self.ups[-1], *values)
        self.downs[-1] = tie(self.downs[-1], *values)

    def blocks(self):
        return self.ups + self.downs[1:]


def weight_quarters(gate_weight, up_weight):
    depth, cols = gate_weight.shape
    return jnp.concatenate(
        [w.T.reshape(Y, cols // Y, depth) for w in (gate_weight, up_weight)], axis=1
    )


def out_partial(out_grad, out_factor):
    half = out_grad.shape[0] // 2
    grads = jnp.pad(out_grad.reshape(2, half, -1), ((0, 0), (0, 256 - half), (0, 0)))
    return lax.dot_general(
        out_factor, grads.reshape(512, -1), (((0,), (1,)), ((), ())),
        preferred_element_type=jnp.float32,
    )


def exchange_z(out, queries):
    rows, cols = queries.shape
    high = lax.reduce_precision(out, 8, 7)
    sent = jnp.concatenate(
        [v.astype(jnp.bfloat16) for v in (high, out - high)] + [queries.reshape(-1, out.shape[1])]
    )
    got = lax.all_gather(sent, "zh")
    count = out.shape[0]
    parts = got[:, : 2 * count].astype(jnp.float32)
    out = (parts[:, :count] + parts[:, count:]).sum(0)
    return out, got[:, 2 * count :].reshape(ZH, rows, cols)


def share_plane(out, queries):
    high = lax.reduce_precision(out, 8, 7)
    sent = jnp.concatenate(
        [v.astype(jnp.bfloat16) for v in (high, out - high)]
        + [queries.reshape(-1, out.shape[1])]
    )
    return lax.all_gather(sent, PLANE)


def unpack_queries(got, first, rows, cols):
    here = got.reshape((Y, X * C) + got.shape[1:])
    here = lax.dynamic_index_in_dim(here, lax.axis_index("y"), 0, keepdims=False)
    queries = here[:, first:].reshape(X, C, ZH, rows, cols)
    return queries.transpose(3, 0, 2, 1, 4).reshape(rows, -1)


def shards(tokens, gate_weight, up_weight, out_grad, in_factor, out_factor, queries):
    rows = tokens.shape[0]
    rank = in_factor.shape[1]
    half = rows // 2
    z, y, c = (lax.axis_index(name) for name in ("zl", "y", "c"))
    mine = lax.dynamic_slice_in_dim(tokens, c * half, half, 0)
    plane_tokens = lax.all_gather(mine, ("y", "c"))
    quarter = in_factor.shape[0] // Y
    factor = lax.dynamic_slice_in_dim(in_factor, y * quarter, quarter, 0).T
    factor = jnp.pad(factor, ((0, 0), (0, 256 - quarter)))

    quarters = weight_quarters(gate_weight, up_weight)
    chain = Chain(lax.all_to_all(quarters, "y", 0, 0, tiled=True))
    out = out_partial(out_grad, out_factor).reshape(X * C, rank // (X * C), -1)
    for s in range(1, ZL):
        chain.step()
        if s == 1:
            out = tie(out, chain.ups[-1])
            out = lax.all_to_all(out, ("x", "c"), 0, 0, tiled=True).sum(0)
        if s == 4:
            chain.after(out)
            out = tie(out, chain.ups[-1])
            out, query_rows = exchange_z(out, queries)
        if s == 5:
            chain.after(out, query_rows)
        if s == 6:
            shared = share_plane(out, query_rows)
            chain.after(out, plane_tokens)
            out = tie(out, chain.ups[-1])
            out = share(out, PLANE, Y * X * C)
    out = out.reshape(Y, rank, -1).transpose(1, 0, 2).reshape(rank, -1)

    place = jnp.stack([z]).astype(jnp.int32)
    in_part = layer(place, factor, chain.blocks(), plane_tokens)
    in_proj = lax.all_to_all(in_part, PLANE, 0, 0, tiled=True)
    in_proj = in_proj.sum(0)

    seqs = Y * rows // LEN
    lane = jnp.arange(in_proj.shape[1])
    token = lane // 256 * half + lane % 256
    mask = (token // LEN)[None, :] == jnp.arange(seqs)[:, None]
    spread = jnp.where(mask[:, None, :], in_proj[None], 0.0).reshape(2 * seqs, -1)
    fragment = jnp.dot(spread, out.T, precision=HIGHEST) / jnp.sqrt(jnp.float32(LEN))
    fragment = fragment.reshape(seqs, 2 * rank)
    columns = share(fragment, ("zh", "zl"), ZH * ZL)
    columns, shared = lax.optimization_barrier((columns, shared))
    columns = columns.reshape(ZH, ZL * seqs, 2 * rank).sum(0).astype(jnp.bfloat16)
    query_rows = unpack_queries(shared, 2 * rank // (X * C), *queries.shape)
    features = share(columns, PLANE, Y * X * C)
    return solve(features, query_rows)


def solution(mesh):
    fine = Mesh(mesh.devices.reshape(ZL, Y, X, ZH, C), ("zl", "y", "x", "zh", "c"))
    dp, tensor = ("zl", "y"), ("x", "zh", "c")
    in_specs = (
        P(dp, None),
        P(dp, tensor),
        P(dp, tensor),
        P(dp, tensor),
        P(tensor, None),
        P(tensor, None),
        P(dp, tensor),
    )
    return jax.shard_map(
        shards, mesh=fine, in_specs=in_specs, out_specs=P(dp, None), check_vma=False
    )
```
